32 devices in a mesh: lat: 2 (over x), lon: 4 (over y, core), mem: 4 (over z).
Axes of the slice: x: 2, y: 2, z: 4, core: 2. Of those that a mesh axis runs over, the one named last changes fastest.
Arguments:
- perturbations: bfloat16 [32, 128, 1024], P('mem', 'lat', 'lon'), may hold values from -6 to 6
- diffusivity: float32 [128, 1024], P('lat', 'lon'), may hold values from 0.19 to 0.249
- sea_mask: int32 [128, 1024], P('lat', 'lon'), may hold values from 0 to 1
- obs_owner: int32 [65536, 1], P(('lat', 'lon', 'mem')), may hold values from 0 to 7; in each aligned block of 2048 rows (0 to 2047, 2048 to 4095, ...) at most 512 rows name the same one
- obs_cell: int32 [65536], P(('lat', 'lon', 'mem')), may hold values from 0 to 16383
- obs_depart: float32 [65536], P(('lat', 'lon', 'mem')), may hold values from -6 to 6
- obs_weight: float32 [65536], P(('lat', 'lon', 'mem')), may hold values from 0.25 to 2
Outputs:
- increment: float32 [128, 1024], P('lat', 'lon')
- obs_residual: float32 [65536], P(('lat', 'lon', 'mem'))
The draws below stay inside these ranges and needn't reach their ends.
Inputs may be any that keep to these rules, and one draw needn't show every extreme that they name: `obs_owner`: within each device's aligned block of 2048 rows no tile is named by more than 512 rows, a bound that some block reaches.
All inputs are finite; a program needn't handle non-finite values.
Results may differ from the reference program's by a relative error of at most 0.0003.
Values sent between devices are 32-bit elements; how exact they have to be, the bound alone decides.
A program may use at most 64 MiB of HBM per device.

```python
import math
import jax
import jax.numpy as jnp
import numpy as np
from jax import lax

LAT_DEV = 64
LON_DEV = 256
STEPS = 4
OBS_DEV = 2048
NLAT = 128
NLON = 1024
MEMBERS = 32
OWNERS = 8
CAP = 512
OBS = 65536


def draw_sea_mask(key, part):
    key = jax.random.fold_in(key, 11)
    grid_rows = jnp.arange(NLAT, dtype=jnp.int32) % LAT_DEV
    grid_cols = jnp.arange(NLON, dtype=jnp.int32) % LON_DEV
    edge_rows = jnp.minimum(grid_rows, LAT_DEV - 1 - grid_rows) < 4
    edge_cols = jnp.minimum(grid_cols, LON_DEV - 1 - grid_cols) < 4
    border = edge_rows[:, None] | edge_cols[None, :]
    dice_values = jax.random.randint(key, (NLAT, NLON), 0, 320, dtype=jnp.int32)
    threshold = jnp.where(border, 5, 64).astype(jnp.int32)
    return jnp.where(dice_values < threshold, 0, 1).astype(jnp.int32)


def place_ends(drawn, own_key, smallest, largest):
    extent = drawn.shape
    spot = [jax.random.randint(jax.random.fold_in(own_key, axis), (), 0, extent[axis]) for axis in range(len(extent))]
    drawn = drawn.at[tuple(spot)].set(smallest)
    longest = extent.index(max(extent))
    spot[longest] = (spot[longest] + 1) % extent[longest]
    return drawn.at[tuple(spot)].set(largest)


def steps_of(key, extent, cuts, least, largest):
    def one(axis_at, shards_of):
        heights = jax.random.uniform(jax.random.fold_in(jax.random.fold_in(key, 6), axis_at), (shards_of,), jnp.float32, least / len(cuts), largest / len(cuts))
        return jnp.repeat(jnp.exp(heights), extent[axis_at] // shards_of).reshape((-1,) + (1,) * (len(extent) - axis_at - 1))

    loudness = one(*cuts[0])
    for cut in cuts[1:]:
        loudness = loudness * one(*cut)
    return loudness


def routed_block(stream_key, own, number, rows, amount, top, reach, skew):
    sequence = jax.random.permutation(stream_key, amount)
    crowded, ordinary = load_shares(amount, rows * top, reach, skew, True), load_shares(amount, rows * top, reach, skew, False)
    places = jnp.arange(amount)

    def named(lengths, turn):
        used = int((lengths > 0).sum())
        fixed = max(1, used // 4)
        moved = fixed + (places - fixed + turn * (used - fixed)) % max(1, amount - fixed)
        return jnp.zeros((amount,), jnp.int32).at[sequence[jnp.where(places < fixed, places, moved)]].set(jnp.asarray(lengths, jnp.int32))

    lengths = jnp.where(number % 4 == 0, named(crowded, number // 4), named(ordinary, number - number // 4 - 1))
    mixed = jax.random.permutation(jax.random.fold_in(own, 3), amount)
    donor, taker = mixed[0:amount // 2 * 2:2], mixed[1:amount // 2 * 2:2]
    margin = jnp.minimum(lengths[donor] - 1, reach - lengths[taker]) // 2
    margin = jnp.where((donor == sequence[0]) | (taker == sequence[0]) | (lengths[taker] == 0), 0, jnp.maximum(margin, 0))
    moved = jax.random.randint(jax.random.fold_in(own, 4), (amount // 2,), 0, 1 << 20) % (margin + 1)
    lengths = lengths.at[donor].add(-moved).at[taker].add(moved)
    labels = jnp.searchsorted(jnp.cumsum(lengths), jnp.arange(rows * top), side="right").astype(jnp.int32)
    table = labels.reshape(top, rows).T
    table = table[jax.random.permutation(jax.random.fold_in(own, 1), rows)]
    turn = jax.random.randint(jax.random.fold_in(own, 2), (rows, 1), 0, top)
    return jnp.take_along_axis(table, (jnp.arange(top)[None, :] + turn) % top, axis=1)


def load_shares(number_of, total, most, slope, full):
    weights = [(1 << 20) // math.isqrt(grade ** slope) + 1 for grade in range(1, number_of + 1)]
    largest = most if full else min(most, max(-(-total // number_of), total * weights[0] // sum(weights)))
    least = 1 if total - largest >= number_of - 1 else 0
    counts, surplus = [largest] + [least] * (number_of - 1), total - largest - least * (number_of - 1)
    while surplus > 0:
        free = [i for i in range(1, number_of) if counts[i] < largest] or [i for i in range(1, number_of) if counts[i] < most]
        whole, left = sum([weights[i] for i in free]), surplus
        for i in free:
            addition = min(most - counts[i], max(1, left * weights[i] // whole), surplus)
            counts[i] = counts[i] + addition
            surplus = surplus - addition
    return np.array(counts)


def centred(key, shape, scale, bound, pieces=(), kind=jnp.bfloat16):
    factor_of = steps_of(key, shape, pieces, -0.22, 0.18) if pieces else 1.0
    drawn = jax.random.normal(key, shape, jnp.float32) * scale * factor_of
    return jnp.minimum(jnp.maximum(drawn, -bound), bound).astype(kind)


def setup_inputs(seed: int = 0) -> dict:
    arg_keys = jax.random.split(jax.random.key(seed), 8)
    perturbations = centred(arg_keys[0], (MEMBERS, NLAT, NLON), 1.0, 6.0, ((0, 4), (1, 2), (2, 4)))
    diffusivity = jnp.clip(0.19 + 0.059 * jax.random.uniform(arg_keys[1], (NLAT, NLON), jnp.float32) ** steps_of(arg_keys[1], (NLAT, NLON), ((0, 2), (1, 4)), -0.2, 0.2), 0.19, 0.249)
    sea_mask = draw_sea_mask(jax.random.fold_in(arg_keys[7], 71), 0)
    obs_owner_keys = jax.random.split(jax.random.fold_in(arg_keys[3], 1), OBS // OBS_DEV)
    obs_owner_turns = jax.random.permutation(jax.random.fold_in(arg_keys[3], 3), OBS // OBS_DEV)
    obs_owner = jax.vmap(lambda own, number: routed_block(jax.random.fold_in(arg_keys[3], 2), own, number, OBS_DEV, OWNERS, 1, CAP, 2))(obs_owner_keys, obs_owner_turns).reshape((OBS, 1))
    obs_cell = place_ends(jax.random.randint(arg_keys[4], (OBS,), 0, LAT_DEV * LON_DEV), jax.random.fold_in(arg_keys[4], 1), 0, (LAT_DEV * LON_DEV) - 1).astype(jnp.int32)
    obs_depart = centred(arg_keys[5], (OBS,), 1.0, 6.0, ((0, 32),), jnp.float32)
    obs_weight = jnp.clip(jnp.exp(math.log(2.0) - 2.0794415 * jax.random.uniform(arg_keys[6], (OBS,), jnp.float32) ** steps_of(arg_keys[6], (OBS,), ((0, 32),), -0.2, 0.2)), 0.25, 2.0)
    return dict(perturbations=perturbations, diffusivity=diffusivity, sea_mask=sea_mask, obs_owner=obs_owner, obs_cell=obs_cell, obs_depart=obs_depart, obs_weight=obs_weight)


def diffuse_once(spread, north_face, east_face):
    flux_north = north_face * (spread[1:] - spread[:-1])
    zero_row = jnp.zeros((1, spread.shape[1]), spread.dtype)
    vertical = jnp.concatenate([flux_north, zero_row], 0) - jnp.concatenate([zero_row, flux_north], 0)
    flux_east = east_face * (jnp.roll(spread, -1, axis=1) - spread)
    return spread + vertical + (flux_east - jnp.roll(flux_east, 1, axis=1))


def covariance(source, perturbations, north_face, east_face, sea_cover):
    def add_member(summed, member):
        member_values = member.astype(jnp.float32)
        spread = member_values * source
        for sweep_index in range(STEPS):
            spread = diffuse_once(spread, north_face, east_face)
        return summed + member_values * spread, None

    summed, unused = lax.scan(add_member, jnp.zeros_like(source), perturbations)
    return sea_cover * summed / (MEMBERS - 1)


def reference(perturbations, diffusivity, sea_mask, obs_owner, obs_cell, obs_depart, obs_weight):
    sea_cover = sea_mask.astype(jnp.float32)
    north_face = 0.5 * (diffusivity[:-1] + diffusivity[1:]) * sea_cover[:-1] * sea_cover[1:]
    rate_next = jnp.roll(diffusivity, -1, axis=1)
    sea_next = jnp.roll(sea_cover, -1, axis=1)
    east_face = 0.5 * (diffusivity + rate_next) * sea_cover * sea_next
    tiles_lon = NLON // LON_DEV
    obs_dest = obs_owner[:, 0]
    grid_row = (obs_dest // tiles_lon) * LAT_DEV + obs_cell // LON_DEV
    grid_col = (obs_dest % tiles_lon) * LON_DEV + obs_cell % LON_DEV
    flat_cell = (grid_row * NLON + grid_col).astype(jnp.int32)
    tile_cells = NLAT * NLON
    innovation = jax.ops.segment_sum(obs_weight * obs_depart, flat_cell, num_segments=tile_cells).reshape(NLAT, NLON)
    first_pass = covariance(innovation, perturbations, north_face, east_face, sea_cover)
    at_obs = first_pass.reshape(-1)[flat_cell]
    removed = jax.ops.segment_sum(obs_weight * at_obs, flat_cell, num_segments=tile_cells).reshape(NLAT, NLON)
    corrected = innovation - removed
    increment = covariance(corrected, perturbations, north_face, east_face, sea_cover)
    obs_residual = obs_depart - increment.reshape(-1)[flat_cell]
    return increment, obs_residual
```

```python
import functools

import jax
import jax.numpy as jnp
from jax import lax
from jax.experimental import pallas as pl
from jax.experimental.pallas import tpu as pltpu
from jax.sharding import PartitionSpec as P

STEPS = 4
LANES = 128
RIM = 8
F32 = jnp.float32
BF16 = jnp.bfloat16
MESH = pl.DeviceIdType.MESH
DIRECTIONS = [(0, 1), (0, -1), (1, 0), (-1, 0), (1, 1), (1, -1), (-1, 1), (-1, -1)]


def halves(value):
    high = value.astype(BF16).astype(F32)
    return high, value - high


def dot_nt(left, right):
    return lax.dot_general(left, right, (((1,), (1,)), ((), ())), preferred_element_type=F32)


def dot_nn(left, right):
    return lax.dot_general(left, right, (((1,), (0,)), ((), ())), preferred_element_type=F32)


def rows_iota(count):
    return lax.broadcasted_iota(jnp.int32, (count, LANES), 0)


def one_hot(index_row, count):
    return jnp.where(rows_iota(count) == index_row, 1.0, 0.0).astype(BF16)


def kernel(
    sizes,
    member_ref, rate_ref, sea_ref, owner_ref, cell_ref, depart_ref, weight_ref,
    increment_ref, residual_ref,
    member_ext, coef_ext, source1, source2, spread, member_all, north_all, east_all,
    outgoing, arrived, partial1, partial, gathered1, gathered2, gathered3, kept, answers, returned,
    rank_ref, total_ref, wide_ref,
    send_x, recv_x, send_c, recv_c, send_v1, recv_v1, send_v2, recv_v2, sums_sem, a2a_sem,
):
    lat_size, lon_size, mem_size, places, q, block_rows, divisor = sizes
    tile_rows, tile_cols = rate_ref.shape
    chunks = owner_ref.shape[0]
    lat = lax.axis_index("lat")
    lon = lax.axis_index("lon")
    mem = lax.axis_index("mem")
    place = lat * lon_size + lon
    quarter = tile_rows // mem_size
    shift_q = q.bit_length() - 1
    shift_b = block_rows.bit_length() - 1
    end = RIM + tile_rows
    ext_rows = tile_rows + 2 * RIM

    def place_at(step):
        other = lax.rem(place + step, places)
        return other, (other // lon_size, lax.rem(other, lon_size), mem)

    barrier = pltpu.get_barrier_semaphore()

    def greet(step, carry):
        pl.semaphore_signal(barrier, inc=1, device_id=place_at(step)[1], device_id_type=MESH)
        return carry

    lax.fori_loop(1, places, greet, 0)
    for step in range(1, mem_size):
        pl.semaphore_signal(
            barrier, inc=1, device_id=(lat, lon, lax.rem(mem + step, mem_size)), device_id_type=MESH
        )

    zero_rows = jnp.zeros((RIM, 512), F32)
    for ext in (source1, source2, coef_ext.at[0], coef_ext.at[1]):
        @pl.when(lat == 0)
        def _(ext=ext):
            ext[0:RIM, :] = zero_rows

        @pl.when(lat == lat_size - 1)
        def _(ext=ext):
            ext[end:ext_rows, :] = zero_rows

    @pl.when(lat == 0)
    def _():
        member_ext[0:RIM] = jnp.zeros((RIM, 8, 512), F32)

    @pl.when(lat == lat_size - 1)
    def _():
        member_ext[end:ext_rows] = jnp.zeros((RIM, 8, 512), F32)

    member_ext[RIM:end, :, 0:tile_cols] = member_ref[...]
    coef_ext[0, RIM:end, 0:tile_cols] = rate_ref[...]
    coef_ext[1, RIM:end, 0:tile_cols] = sea_ref[...].astype(F32)

    pl.semaphore_wait(barrier, places - 1 + mem_size - 1)

    def halo_copies(at, send_sem, recv_sem):
        made = []
        for k, (dy, dx) in enumerate(DIRECTIONS):
            source_rows = {0: pl.ds(RIM, tile_rows), 1: pl.ds(end - RIM, RIM), -1: pl.ds(RIM, RIM)}[dy]
            target_rows = {0: pl.ds(RIM, tile_rows), 1: pl.ds(0, RIM), -1: pl.ds(end, RIM)}[dy]
            source_cols = {0: pl.ds(0, 256), 1: pl.ds(128, 128), -1: pl.ds(0, 128)}[dx]
            target_cols = {0: pl.ds(0, 256), 1: pl.ds(384, 128), -1: pl.ds(256, 128)}[dx]
            copy = pltpu.make_async_remote_copy(
                src_ref=at(source_rows, source_cols),
                dst_ref=at(target_rows, target_cols),
                send_sem=send_sem.at[k],
                recv_sem=recv_sem.at[k],
                device_id=(lat + dy, lax.rem(lon + dx + lon_size, lon_size), mem),
                device_id_type=MESH,
            )
            sends = {0: None, 1: lat < lat_size - 1, -1: lat > 0}[dy]
            gets = {0: None, 1: lat > 0, -1: lat < lat_size - 1}[dy]
            made.append((copy, sends, gets))
        return made

    def when(condition, action):
        if condition is None:
            action()
        else:
            pl.when(condition)(action)

    def halo_start(copies):
        for copy, sends, gets in copies:
            when(sends, lambda copy=copy: copy.start())

    def halo_wait(copies):
        for copy, sends, gets in copies:
            when(sends, lambda copy=copy: copy.wait_send())
            when(gets, lambda copy=copy: copy.wait_recv())

    coef_copies = halo_copies(lambda r, c: coef_ext.at[:, r, c], send_c, recv_c)
    member_copies = halo_copies(lambda r, c: member_ext.at[r, :, c], send_x, recv_x)
    source_copies = [
        halo_copies(lambda r, c: source1.at[r, c], send_v1, recv_v1),
        halo_copies(lambda r, c: source2.at[r, c], send_v2, recv_v2),
    ]

    owner = owner_ref[...]
    upper = jnp.where(
        lax.broadcasted_iota(jnp.int32, (LANES, LANES), 0)
        < lax.broadcasted_iota(jnp.int32, (LANES, LANES), 1), 1.0, 0.0,
    ).astype(BF16)
    table = jnp.concatenate([upper, jnp.ones((LANES, LANES), BF16)], axis=1)
    before = jnp.zeros((places, LANES), F32)
    for r in range(chunks):
        match = one_hot(owner[r : r + 1], places)
        counts = dot_nn(match, table)
        found = jnp.sum(match.astype(F32) * (counts[:, :LANES] + before), axis=0, keepdims=True)
        rank_ref[r : r + 1, :] = found.astype(jnp.int32)
        before = before + counts[:, LANES:]
    rank = rank_ref[...]
    slot_row = owner * block_rows + lax.shift_right_logical(rank, 7)
    slot_lane = lax.bitwise_and(rank, 127)

    depart = depart_ref[...]
    weight = weight_ref[...]
    cell = cell_ref[...]
    product1, product2 = halves(weight * depart)
    weight1, weight2 = halves(weight)
    cell2 = lax.bitwise_and(cell, 127)
    cell1 = (cell - cell2).astype(F32)
    cell2 = cell2.astype(F32)
    pack_rows = places * block_rows
    row = rows_iota(pack_rows)
    inner = lax.bitwise_and(row, block_rows - 1)
    field = lax.shift_right_logical(inner, shift_q)
    base_row = row - lax.shift_left(field, shift_q)
    packed = jnp.zeros((pack_rows, LANES), F32)
    for r in range(0, chunks, 2):
        lefts1, lefts2, rights = [], [], []
        for c in (r, r + 1):
            s = slice(c, c + 1)
            hit = base_row == slot_row[s]
            lefts1.append(jnp.where(hit, jnp.where(field == 0, product1[s], jnp.where(field == 1, weight1[s], jnp.where(field == 2, cell1[s], 0.0))), 0.0).astype(BF16))
            lefts2.append(jnp.where(hit, jnp.where(field == 0, product2[s], jnp.where(field == 1, weight2[s], jnp.where(field == 2, cell2[s], 0.0))), 0.0).astype(BF16))
            rights.append(one_hot(slot_lane[s], LANES))
        right = jnp.concatenate(rights, axis=1)
        packed = packed + dot_nt(jnp.concatenate(lefts1, axis=1), right)
        packed = packed + dot_nt(jnp.concatenate(lefts2, axis=1), right)
    outgoing[...] = packed.reshape(places, block_rows, LANES)

    def exchange(from_ref, to_ref, sems):
        def send(step, carry):
            other, device = place_at(step)
            pltpu.make_async_remote_copy(
                src_ref=from_ref.at[other], dst_ref=to_ref.at[place],
                send_sem=sems.at[0], recv_sem=sems.at[1],
                device_id=device, device_id_type=MESH,
            ).start()
            return carry

        lax.fori_loop(1, places, send, 0)

    def exchange_wait(from_ref, to_ref, sems):
        whole = pltpu.make_async_remote_copy(
            src_ref=from_ref.at[pl.ds(0, places - 1)], dst_ref=to_ref.at[pl.ds(0, places - 1)],
            send_sem=sems.at[0], recv_sem=sems.at[1],
            device_id=place_at(1)[1], device_id_type=MESH,
        )
        whole.wait_send()
        whole.wait_recv()

    exchange(outgoing, arrived, a2a_sem.at[0])
    halo_start(coef_copies)
    halo_start(member_copies)
    arrived[place] = outgoing[place]
    exchange_wait(outgoing, arrived, a2a_sem.at[0])

    def slot_cells(block):
        whole = block[2 * q : 3 * q].astype(jnp.int32)
        lane = lax.bitwise_and(whole, 127)
        half = lax.bitwise_and(lax.shift_right_logical(whole, 7), 1)
        return lax.shift_right_logical(whole, 8) + half * tile_rows, lane

    halves_rows = 2 * tile_rows
    total_ref[...] = jnp.zeros_like(total_ref)

    def add_block(origin, carry):
        block = arrived[origin]
        high, lane = slot_cells(block)
        lefts, rights = [], []
        for k in range(q):
            hit = rows_iota(halves_rows) == high[k : k + 1]
            parts = halves(block[k : k + 1]) + halves(block[q + k : q + k + 1])
            lefts.append(jnp.concatenate([jnp.where(hit, part, 0.0).astype(BF16) for part in parts], axis=0))
            rights.append(one_hot(lane[k : k + 1], LANES))
        total_ref[...] += dot_nt(jnp.concatenate(lefts, axis=1), jnp.concatenate(rights, axis=1))
        return carry

    lax.fori_loop(0, places, add_block, 0)
    h = halves_rows
    for f in range(2):
        both = total_ref[2 * f * h : (2 * f + 1) * h, :] + total_ref[(2 * f + 1) * h : (2 * f + 2) * h, :]
        partial1[f, :, 0:LANES] = both[:tile_rows]
        partial1[f, :, LANES : 2 * LANES] = both[tile_rows:]

    my_rows = pl.multiple_of(mem * quarter, quarter)

    def member_sum(part_at, got, number):
        sems = sums_sem.at[2 * number]
        for step in range(1, mem_size):
            other = lax.rem(mem + step, mem_size)
            pltpu.make_async_remote_copy(
                src_ref=part_at(pl.ds(pl.multiple_of(other * quarter, quarter), quarter)),
                dst_ref=got.at[mem],
                send_sem=sems.at[0], recv_sem=sems.at[1],
                device_id=(lat, lon, other), device_id_type=MESH,
            ).start()
        got[mem] = part_at(pl.ds(my_rows, quarter))[...]
        whole = pltpu.make_async_remote_copy(
            src_ref=got.at[pl.ds(0, mem_size - 1)], dst_ref=got.at[pl.ds(0, mem_size - 1)],
            send_sem=sems.at[0], recv_sem=sems.at[1],
            device_id=(lat, lon, lax.rem(mem + 1, mem_size)), device_id_type=MESH,
        )
        whole.wait_send()
        whole.wait_recv()
        total = got[0]
        for other in range(1, mem_size):
            total = total + got[other]
        return total

    def member_share(ref, first, number):
        sems = sums_sem.at[2 * number + 1]
        mine = ref.at[pl.ds(first + my_rows, quarter), pl.ds(0, tile_cols)]
        for step in range(1, mem_size):
            pltpu.make_async_remote_copy(
                src_ref=mine, dst_ref=mine,
                send_sem=sems.at[0], recv_sem=sems.at[1],
                device_id=(lat, lon, lax.rem(mem + step, mem_size)), device_id_type=MESH,
            ).start()
        rest = ref.at[pl.ds(first, (mem_size - 1) * quarter), pl.ds(0, tile_cols)]
        whole = pltpu.make_async_remote_copy(
            src_ref=rest, dst_ref=rest, send_sem=sems.at[0], recv_sem=sems.at[1],
            device_id=(lat, lon, lax.rem(mem + 1, mem_size)), device_id_type=MESH,
        )
        whole.wait_send()
        whole.wait_recv()

    summed = member_sum(lambda rows: partial1.at[:, rows], gathered1, 0)
    kept[...] = summed
    source1[pl.ds(RIM + my_rows, quarter), 0:tile_cols] = summed[0]
    member_share(source1, RIM, 0)
    halo_start(source_copies[0])

    lane = lax.broadcasted_iota(jnp.int32, (1, LANES), 1)

    def joined(value):
        side = jnp.where(lane < 64, value[..., 256:384], value[..., 384:512])
        return jnp.concatenate([value[..., 0:256], side], axis=-1)

    halo_wait(coef_copies)
    halo_wait(member_copies)
    rate = joined(coef_ext[0])
    sea = joined(coef_ext[1])
    below = lambda a: jnp.concatenate([a[1:], a[:1]], axis=0)
    width = 384
    wide_ref[0] = 0.5 * (rate + below(rate)) * sea * below(sea)
    wide_ref[1] = 0.5 * (rate + pltpu.roll(rate, width - 1, 1)) * sea * pltpu.roll(sea, width - 1, 1)

    def widen(step, carry):
        base = pl.multiple_of(step * 8, 8)
        for u in range(8):
            i = base + u
            north_all[i] = jnp.broadcast_to(wide_ref[0, pl.ds(i, 1), :], (8, width))
            east_all[i] = jnp.broadcast_to(wide_ref[1, pl.ds(i, 1), :], (8, width))
            value = member_ext[i]
            side = jnp.where(lane < 64, value[:, 256:384], value[:, 384:512])
            member_all[i, :, 0:256] = value[:, 0:256]
            member_all[i, :, 256:384] = side
        return carry

    lax.fori_loop(0, ext_rows // 8, widen, 0)

    def covariance(source):
        wide_ref[0] = joined(source[...])

        def sweep(read, write):
            at = read(3)
            here = read(4)

            def rows(step, carry):
                here, flux = carry
                for u in range(8):
                    i = 4 + step * 8 + u
                    after = read(i + 1)
                    flux_after = north_all[i] * (after - here)
                    flux_east = east_all[i] * (pltpu.roll(here, width - 1, 1) - here)
                    write(i, here + (flux_after - flux) + (flux_east - pltpu.roll(flux_east, 1, 1)))
                    here, flux = after, flux_after
                return here, flux

            lax.fori_loop(0, (tile_rows + 8) // 8, rows, (here, north_all[3] * (here - at)))

        def begin(i):
            return member_all[i] * wide_ref[0, pl.ds(i, 1), :]

        def keep(i, value):
            spread[i] = value

        spread[3] = begin(3)
        spread[tile_rows + 12] = begin(tile_rows + 12)
        sweep(begin, keep)
        for turn in range(STEPS - 1):
            sweep(lambda i: spread[i], keep)

        def collect(step, carry):
            base = pl.multiple_of(step * 8, 8)
            found = [
                jnp.sum(spread[RIM + base + u, :, 0:256] * member_all[RIM + base + u, :, 0:256], axis=0, keepdims=True)
                for u in range(8)
            ]
            partial[pl.ds(base, 8), :] = jnp.concatenate(found, axis=0)
            return carry

        lax.fori_loop(0, tile_rows // 8, collect, 0)

    my_sea = lambda: coef_ext[1, pl.ds(RIM + my_rows, quarter), 0:tile_cols]
    halo_wait(source_copies[0])
    covariance(source1)
    first_pass = my_sea() * member_sum(lambda rows: partial.at[rows], gathered2, 1) / divisor
    source2[pl.ds(RIM + my_rows, quarter), 0:tile_cols] = kept[0] - kept[1] * first_pass
    member_share(source2, RIM, 1)
    halo_start(source_copies[1])
    halo_wait(source_copies[1])
    covariance(source2)
    wide = my_sea() * member_sum(lambda rows: partial.at[rows], gathered3, 2) / divisor
    increment_ref[pl.ds(my_rows, quarter), :] = wide
    member_share(increment_ref, 0, 2)

    field_value = increment_ref[...]
    stacked = jnp.concatenate([field_value[:, :LANES], field_value[:, LANES:]], axis=0)
    first, second = halves(stacked)
    lookup = jnp.concatenate([first, second], axis=0).astype(BF16)

    def look(origin, carry):
        high, lane_of = slot_cells(arrived[origin])
        found = []
        for k in range(q):
            got = dot_nn(lookup, one_hot(lane_of[k : k + 1], LANES))
            value = got[:halves_rows] + got[halves_rows:]
            hit = rows_iota(halves_rows) == high[k : k + 1]
            found.append(jnp.sum(jnp.where(hit, value, 0.0), axis=0, keepdims=True))
        found.append(jnp.zeros((8 - q, LANES), F32))
        answers[origin] = jnp.concatenate(found, axis=0)
        return carry

    lax.fori_loop(0, places, look, 0)
    exchange(answers, returned, a2a_sem.at[1])
    returned[place] = answers[place]
    exchange_wait(answers, returned, a2a_sem.at[1])
    first, second = halves(returned[...].reshape(places * 8, LANES))
    lookup = jnp.concatenate([first, second], axis=0).astype(BF16)
    answer_row = owner * 8 + lax.shift_right_logical(rank_ref[...], 7)
    answer_lane = lax.bitwise_and(rank_ref[...], 127)
    for r in range(chunks):
        got = dot_nn(lookup, one_hot(answer_lane[r : r + 1], LANES))
        value = got[: places * 8] + got[places * 8 :]
        hit = rows_iota(places * 8) == answer_row[r : r + 1]
        found = jnp.sum(jnp.where(hit, value, 0.0), axis=0, keepdims=True)
        residual_ref[r : r + 1, :] = depart_ref[r : r + 1, :] - found


def per_device(sizes, perturbations, diffusivity, sea_mask, obs_owner, obs_cell, obs_depart, obs_weight):
    lat_size, lon_size, mem_size = sizes
    members, tile_rows, tile_cols = perturbations.shape
    count = obs_cell.shape[0]
    places = lat_size * lon_size
    capacity = max(2, 2 * count // places)
    q = max(1, capacity // LANES)
    block_rows = 8
    while block_rows < 3 * q:
        block_rows *= 2
    rows = count // LANES
    ext = tile_rows + 2 * RIM
    quarter = tile_rows // mem_size
    divisor = members * mem_size - 1
    vmem = pltpu.VMEM
    dma = pltpu.SemaphoreType.DMA
    as_rows = lambda a: a.reshape(rows, LANES)
    member_rows = jnp.transpose(perturbations, (1, 0, 2)).astype(F32)
    increment, residual = pl.pallas_call(
        functools.partial(kernel, (lat_size, lon_size, mem_size, places, q, block_rows, divisor)),
        out_shape=(
            jax.ShapeDtypeStruct((tile_rows, tile_cols), F32),
            jax.ShapeDtypeStruct((rows, LANES), F32),
        ),
        in_specs=[pl.BlockSpec(memory_space=vmem)] * 7,
        out_specs=(pl.BlockSpec(memory_space=vmem),) * 2,
        scratch_shapes=[
            vmem((ext, 8, 512), F32),
            vmem((2, ext, 512), F32),
            vmem((ext, 512), F32),
            vmem((ext, 512), F32),
            vmem((ext, 8, 384), F32),
            vmem((ext, 8, 384), F32),
            vmem((ext, 8, 384), F32),
            vmem((ext, 8, 384), F32),
            vmem((places, block_rows, LANES), F32),
            vmem((places, block_rows, LANES), F32),
            vmem((2, tile_rows, tile_cols), F32),
            vmem((tile_rows, tile_cols), F32),
            vmem((mem_size, 2, quarter, tile_cols), F32),
            vmem((mem_size, quarter, tile_cols), F32),
            vmem((mem_size, quarter, tile_cols), F32),
            vmem((2, quarter, tile_cols), F32),
            vmem((places, 8, LANES), F32),
            vmem((places, 8, LANES), F32),
            vmem((rows, LANES), jnp.int32),
            vmem((8 * tile_rows, LANES), F32),
            vmem((2, ext, 384), F32),
        ] + [dma((8,))] * 8 + [dma((6, 2)), dma((2, 2))],
        compiler_params=pltpu.CompilerParams(
            collective_id=0, has_side_effects=True, vmem_limit_bytes=40 * 1024 * 1024
        ),
        name="update",
    )(
        member_rows, diffusivity, sea_mask,
        as_rows(obs_owner), as_rows(obs_cell), as_rows(obs_depart), as_rows(obs_weight),
    )
    return increment, residual.reshape(count)


def solution(mesh):
    sizes = tuple(mesh.shape[name] for name in ("lat", "lon", "mem"))
    return jax.shard_map(
        functools.partial(per_device, sizes),
        mesh=mesh,
        in_specs=(
            P("mem", "lat", "lon"),
            P("lat", "lon"),
            P("lat", "lon"),
            P(("lat", "lon", "mem"), None),
            P(("lat", "lon", "mem")),
            P(("lat", "lon", "mem")),
            P(("lat", "lon", "mem")),
        ),
        out_specs=(P("lat", "lon"), P(("lat", "lon", "mem"))),
        check_vma=False,
    )
```

```python
import functools

import jax
import jax.numpy as jnp
from jax import lax
from jax.experimental import pallas as pl
from jax.experimental.pallas import tpu as pltpu
from jax.sharding import PartitionSpec as P

STEPS = 4
LANES = 128
RIM = 8
F32 = jnp.float32
BF16 = jnp.bfloat16
MESH = pl.DeviceIdType.MESH
DIRECTIONS = [(0, 1), (0, -1), (1, 0), (-1, 0), (1, 1), (1, -1), (-1, 1), (-1, -1)]


def halves(value):
    high = value.astype(BF16).astype(F32)
    return high, value - high


def dot_nt(left, right):
    return lax.dot_general(left, right, (((1,), (1,)), ((), ())), preferred_element_type=F32)


def dot_nn(left, right):
    return lax.dot_general(left, right, (((1,), (0,)), ((), ())), preferred_element_type=F32)


def rows_iota(count):
    return lax.broadcasted_iota(jnp.int32, (count, LANES), 0)


def one_hot(index_row, count):
    return jnp.where(rows_iota(count) == index_row, 1.0, 0.0).astype(BF16)


def kernel(
    sizes,
    member_ref, rate_ref, sea_ref, owner_ref, cell_ref, depart_ref, weight_ref,
    increment_ref, residual_ref,
    member_ext, coef_ext, source1, source2, spread, member_all, north_all, east_all,
    outgoing, arrived, partial1, partial, gathered1, gathered2, gathered3, kept, answers, returned,
    rank_ref, total_ref, wide_ref,
    send_x, recv_x, send_c, recv_c, send_v1, recv_v1, send_v2, recv_v2, sums_sem, a2a_sem,
):
    lat_size, lon_size, mem_size, places, q, block_rows, divisor = sizes
    tile_rows, tile_cols = rate_ref.shape
    chunks = owner_ref.shape[0]
    lat = lax.axis_index("lat")
    lon = lax.axis_index("lon")
    mem = lax.axis_index("mem")
    place = lat * lon_size + lon
    quarter = tile_rows // mem_size
    shift_q = q.bit_length() - 1
    shift_b = block_rows.bit_length() - 1
    end = RIM + tile_rows
    ext_rows = tile_rows + 2 * RIM

    def place_at(step):
        other = lax.rem(place + step, places)
        return other, (other // lon_size, lax.rem(other, lon_size), mem)

    barrier = pltpu.get_barrier_semaphore()

    def greet(step, carry):
        pl.semaphore_signal(barrier, inc=1, device_id=place_at(step)[1], device_id_type=MESH)
        return carry

    lax.fori_loop(1, places, greet, 0)
    for step in range(1, mem_size):
        pl.semaphore_signal(
            barrier, inc=1, device_id=(lat, lon, lax.rem(mem + step, mem_size)), device_id_type=MESH
        )

    zero_rows = jnp.zeros((RIM, 512), F32)
    for ext in (source1, source2, coef_ext.at[0], coef_ext.at[1]):
        @pl.when(lat == 0)
        def _(ext=ext):
            ext[0:RIM, :] = zero_rows

        @pl.when(lat == lat_size - 1)
        def _(ext=ext):
            ext[end:ext_rows, :] = zero_rows

    @pl.when(lat == 0)
    def _():
        member_ext[0:RIM] = jnp.zeros((RIM, 8, 512), F32)

    @pl.when(lat == lat_size - 1)
    def _():
        member_ext[end:ext_rows] = jnp.zeros((RIM, 8, 512), F32)

    member_ext[RIM:end, :, 0:tile_cols] = member_ref[...]
    coef_ext[0, RIM:end, 0:tile_cols] = rate_ref[...]
    coef_ext[1, RIM:end, 0:tile_cols] = sea_ref[...].astype(F32)

    pl.semaphore_wait(barrier, places - 1 + mem_size - 1)

    def halo_copies(at, send_sem, recv_sem):
        made = []
        for k, (dy, dx) in enumerate(DIRECTIONS):
            source_rows = {0: pl.ds(RIM, tile_rows), 1: pl.ds(end - RIM, RIM), -1: pl.ds(RIM, RIM)}[dy]
            target_rows = {0: pl.ds(RIM, tile_rows), 1: pl.ds(0, RIM), -1: pl.ds(end, RIM)}[dy]
            source_cols = {0: pl.ds(0, 256), 1: pl.ds(128, 128), -1: pl.ds(0, 128)}[dx]
            target_cols = {0: pl.ds(0, 256), 1: pl.ds(384, 128), -1: pl.ds(256, 128)}[dx]
            copy = pltpu.make_async_remote_copy(
                src_ref=at(source_rows, source_cols),
                dst_ref=at(target_rows, target_cols),
                send_sem=send_sem.at[k],
                recv_sem=recv_sem.at[k],
                device_id=(lat + dy, lax.rem(lon + dx + lon_size, lon_size), mem),
                device_id_type=MESH,
            )
            sends = {0: None, 1: lat < lat_size - 1, -1: lat > 0}[dy]
            gets = {0: None, 1: lat > 0, -1: lat < lat_size - 1}[dy]
            made.append((copy, sends, gets))
        return made

    def when(condition, action):
        if condition is None:
            action()
        else:
            pl.when(condition)(action)

    def halo_start(copies):
        for copy, sends, gets in copies:
            when(sends, lambda copy=copy: copy.start())

    def halo_wait(copies):
        for copy, sends, gets in copies:
            when(sends, lambda copy=copy: copy.wait_send())
            when(gets, lambda copy=copy: copy.wait_recv())

    coef_copies = halo_copies(lambda r, c: coef_ext.at[:, r, c], send_c, recv_c)
    member_copies = halo_copies(lambda r, c: member_ext.at[r, :, c], send_x, recv_x)
    source_copies = [
        halo_copies(lambda r, c: source1.at[r, c], send_v1, recv_v1),
        halo_copies(lambda r, c: source2.at[r, c], send_v2, recv_v2),
    ]

    owner = owner_ref[...]
    upper = jnp.where(
        lax.broadcasted_iota(jnp.int32, (LANES, LANES), 0)
        < lax.broadcasted_iota(jnp.int32, (LANES, LANES), 1), 1.0, 0.0,
    ).astype(BF16)
    table = jnp.concatenate([upper, jnp.ones((LANES, LANES), BF16)], axis=1)
    before = jnp.zeros((places, LANES), F32)
    for r in range(chunks):
        match = one_hot(owner[r : r + 1], places)
        counts = dot_nn(match, table)
        found = jnp.sum(match.astype(F32) * (counts[:, :LANES] + before), axis=0, keepdims=True)
        rank_ref[r : r + 1, :] = found.astype(jnp.int32)
        before = before + counts[:, LANES:]
    rank = rank_ref[...]
    slot_row = owner * block_rows + lax.shift_right_logical(rank, 7)
    slot_lane = lax.bitwise_and(rank, 127)

    depart = depart_ref[...]
    weight = weight_ref[...]
    cell = cell_ref[...]
    product1, product2 = halves(weight * depart)
    weight1, weight2 = halves(weight)
    cell2 = lax.bitwise_and(cell, 127)
    cell1 = (cell - cell2).astype(F32)
    cell2 = cell2.astype(F32)
    pack_rows = places * block_rows
    row = rows_iota(pack_rows)
    inner = lax.bitwise_and(row, block_rows - 1)
    field = lax.shift_right_logical(inner, shift_q)
    base_row = row - lax.shift_left(field, shift_q)
    packed = jnp.zeros((pack_rows, LANES), F32)
    for r in range(0, chunks, 2):
        lefts1, lefts2, rights = [], [], []
        for c in (r, r + 1):
            s = slice(c, c + 1)
            hit = base_row == slot_row[s]
            lefts1.append(jnp.where(hit, jnp.where(field == 0, product1[s], jnp.where(field == 1, weight1[s], jnp.where(field == 2, cell1[s], 0.0))), 0.0).astype(BF16))
            lefts2.append(jnp.where(hit, jnp.where(field == 0, product2[s], jnp.where(field == 1, weight2[s], jnp.where(field == 2, cell2[s], 0.0))), 0.0).astype(BF16))
            rights.append(one_hot(slot_lane[s], LANES))
        right = jnp.concatenate(rights, axis=1)
        packed = packed + dot_nt(jnp.concatenate(lefts1, axis=1), right)
        packed = packed + dot_nt(jnp.concatenate(lefts2, axis=1), right)
    outgoing[...] = packed.reshape(places, block_rows, LANES)

    def exchange(from_ref, to_ref, sems):
        def send(step, carry):
            other, device = place_at(step)
            pltpu.make_async_remote_copy(
                src_ref=from_ref.at[other], dst_ref=to_ref.at[place],
                send_sem=sems.at[0], recv_sem=sems.at[1],
                device_id=device, device_id_type=MESH,
            ).start()
            return carry

        lax.fori_loop(1, places, send, 0)

    def exchange_wait(from_ref, to_ref, sems):
        whole = pltpu.make_async_remote_copy(
            src_ref=from_ref.at[pl.ds(0, places - 1)], dst_ref=to_ref.at[pl.ds(0, places - 1)],
            send_sem=sems.at[0], recv_sem=sems.at[1],
            device_id=place_at(1)[1], device_id_type=MESH,
        )
        whole.wait_send()
        whole.wait_recv()

    exchange(outgoing, arrived, a2a_sem.at[0])
    halo_start(coef_copies)
    halo_start(member_copies)
    arrived[place] = outgoing[place]
    exchange_wait(outgoing, arrived, a2a_sem.at[0])

    def slot_cells(block):
        whole = block[2 * q : 3 * q].astype(jnp.int32)
        lane = lax.bitwise_and(whole, 127)
        half = lax.bitwise_and(lax.shift_right_logical(whole, 7), 1)
        return lax.shift_right_logical(whole, 8) + half * tile_rows, lane

    halves_rows = 2 * tile_rows
    total_ref[...] = jnp.zeros_like(total_ref)

    def add_block(origin, carry):
        block = arrived[origin]
        high, lane = slot_cells(block)
        lefts, rights = [], []
        for k in range(q):
            hit = rows_iota(halves_rows) == high[k : k + 1]
            parts = halves(block[k : k + 1]) + halves(block[q + k : q + k + 1])
            lefts.append(jnp.concatenate([jnp.where(hit, part, 0.0).astype(BF16) for part in parts], axis=0))
            rights.append(one_hot(lane[k : k + 1], LANES))
        total_ref[...] += dot_nt(jnp.concatenate(lefts, axis=1), jnp.concatenate(rights, axis=1))
        return carry

    lax.fori_loop(0, places, add_block, 0)
    h = halves_rows
    for f in range(2):
        both = total_ref[2 * f * h : (2 * f + 1) * h, :] + total_ref[(2 * f + 1) * h : (2 * f + 2) * h, :]
        partial1[f, :, 0:LANES] = both[:tile_rows]
        partial1[f, :, LANES : 2 * LANES] = both[tile_rows:]

    my_rows = pl.multiple_of(mem * quarter, quarter)

    def sum_copy(part_at, got, number, other):
        sems = sums_sem.at[2 * number]
        return pltpu.make_async_remote_copy(
            src_ref=part_at(pl.ds(pl.multiple_of(other * quarter, quarter), quarter)),
            dst_ref=got.at[mem],
            send_sem=sems.at[0], recv_sem=sems.at[1],
            device_id=(lat, lon, other), device_id_type=MESH,
        )

    def sum_part(part_at, got, number, other):
        @pl.when(mem != other)
        def _():
            sum_copy(part_at, got, number, other).start()

    def member_sum(part_at, got, number):
        sems = sums_sem.at[2 * number]
        got[mem] = part_at(pl.ds(my_rows, quarter))[...]
        whole = pltpu.make_async_remote_copy(
            src_ref=got.at[pl.ds(0, mem_size - 1)], dst_ref=got.at[pl.ds(0, mem_size - 1)],
            send_sem=sems.at[0], recv_sem=sems.at[1],
            device_id=(lat, lon, lax.rem(mem + 1, mem_size)), device_id_type=MESH,
        )
        whole.wait_send()
        whole.wait_recv()
        total = got[0]
        for other in range(1, mem_size):
            total = total + got[other]
        return total

    def member_share(ref, first, number):
        sems = sums_sem.at[2 * number + 1]
        mine = ref.at[pl.ds(first + my_rows, quarter), pl.ds(0, tile_cols)]
        for step in range(1, mem_size):
            pltpu.make_async_remote_copy(
                src_ref=mine, dst_ref=mine,
                send_sem=sems.at[0], recv_sem=sems.at[1],
                device_id=(lat, lon, lax.rem(mem + step, mem_size)), device_id_type=MESH,
            ).start()
        rest = ref.at[pl.ds(first, (mem_size - 1) * quarter), pl.ds(0, tile_cols)]
        whole = pltpu.make_async_remote_copy(
            src_ref=rest, dst_ref=rest, send_sem=sems.at[0], recv_sem=sems.at[1],
            device_id=(lat, lon, lax.rem(mem + 1, mem_size)), device_id_type=MESH,
        )
        whole.wait_send()
        whole.wait_recv()

    first_part = lambda rows: partial1.at[:, rows]
    for step in range(1, mem_size):
        sum_copy(first_part, gathered1, 0, lax.rem(mem + step, mem_size)).start()
    summed = member_sum(first_part, gathered1, 0)
    kept[...] = summed
    source1[pl.ds(RIM + my_rows, quarter), 0:tile_cols] = summed[0]
    member_share(source1, RIM, 0)
    halo_start(source_copies[0])

    lane = lax.broadcasted_iota(jnp.int32, (1, LANES), 1)

    def joined(value):
        side = jnp.where(lane < 64, value[..., 256:384], value[..., 384:512])
        return jnp.concatenate([value[..., 0:256], side], axis=-1)

    halo_wait(coef_copies)
    halo_wait(member_copies)
    rate = joined(coef_ext[0])
    sea = joined(coef_ext[1])
    below = lambda a: jnp.concatenate([a[1:], a[:1]], axis=0)
    width = 384
    wide_ref[0] = 0.5 * (rate + below(rate)) * sea * below(sea)
    wide_ref[1] = 0.5 * (rate + pltpu.roll(rate, width - 1, 1)) * sea * pltpu.roll(sea, width - 1, 1)

    def widen(step, carry):
        base = pl.multiple_of(step * 8, 8)
        for u in range(8):
            i = base + u
            north_all[i] = jnp.broadcast_to(wide_ref[0, pl.ds(i, 1), :], (8, width))
            east_all[i] = jnp.broadcast_to(wide_ref[1, pl.ds(i, 1), :], (8, width))
            value = member_ext[i]
            side = jnp.where(lane < 64, value[:, 256:384], value[:, 384:512])
            member_all[i, :, 0:256] = value[:, 0:256]
            member_all[i, :, 256:384] = side
        return carry

    lax.fori_loop(0, ext_rows // 8, widen, 0)

    def covariance(source, finished):
        wide_ref[0] = joined(source[...])

        def step_rows(read, base, carry, count):
            here, flux = carry
            values = [here] + [read(base + u + 1) for u in range(count)]
            results = []
            for u in range(count):
                here, after = values[u], values[u + 1]
                flux_after = north_all[base + u] * (after - here)
                flux_east = east_all[base + u] * (pltpu.roll(here, width - 1, 1) - here)
                results.append(here + (flux_after - flux) + (flux_east - pltpu.roll(flux_east, 1, 1)))
                flux = flux_after
            return results, (values[-1], flux)

        def first_of(read, row):
            here = read(row)
            return here, north_all[row - 1] * (here - read(row - 1))

        def sweep(read):
            def rows(step, carry):
                base = 4 + step * 8
                results, carry = step_rows(read, base, carry, 8)
                for u in range(8):
                    spread[base + u] = results[u]
                return carry

            lax.fori_loop(0, (tile_rows + 8) // 8, rows, first_of(read, 4))

        def begin(i):
            return member_all[i] * wide_ref[0, pl.ds(i, 1), :]

        def again(i):
            return spread[i]

        spread[3] = begin(3)
        spread[tile_rows + 12] = begin(tile_rows + 12)
        sweep(begin)
        for turn in range(STEPS - 2):
            sweep(again)

        def last_rows(step, carry):
            base = RIM + step * 8
            results, carry = step_rows(again, base, carry, 8)
            found = [
                jnp.sum(results[u][:, 0:256] * member_all[base + u, :, 0:256], axis=0, keepdims=True)
                for u in range(8)
            ]
            partial[pl.ds(pl.multiple_of(step * 8, 8), 8), :] = jnp.concatenate(found, axis=0)
            return carry

        carry = first_of(again, RIM)
        steps = quarter // 8
        for part in range(mem_size):
            carry = lax.fori_loop(part * steps, (part + 1) * steps, last_rows, carry)
            finished(part)

    my_sea = lambda: coef_ext[1, pl.ds(RIM + my_rows, quarter), 0:tile_cols]
    halo_wait(source_copies[0])
    later_part = lambda rows: partial.at[rows]
    covariance(source1, lambda part: sum_part(later_part, gathered2, 1, part))
    first_pass = my_sea() * member_sum(later_part, gathered2, 1) / divisor
    source2[pl.ds(RIM + my_rows, quarter), 0:tile_cols] = kept[0] - kept[1] * first_pass
    member_share(source2, RIM, 1)
    halo_start(source_copies[1])
    halo_wait(source_copies[1])
    covariance(source2, lambda part: sum_part(later_part, gathered3, 2, part))
    wide = my_sea() * member_sum(later_part, gathered3, 2) / divisor
    increment_ref[pl.ds(my_rows, quarter), :] = wide
    member_share(increment_ref, 0, 2)

    field_value = increment_ref[...]
    stacked = jnp.concatenate([field_value[:, :LANES], field_value[:, LANES:]], axis=0)
    first, second = halves(stacked)
    lookup = jnp.concatenate([first, second], axis=0).astype(BF16)

    def look(origin, carry):
        high, lane_of = slot_cells(arrived[origin])
        found = []
        for k in range(q):
            got = dot_nn(lookup, one_hot(lane_of[k : k + 1], LANES))
            value = got[:halves_rows] + got[halves_rows:]
            hit = rows_iota(halves_rows) == high[k : k + 1]
            found.append(jnp.sum(jnp.where(hit, value, 0.0), axis=0, keepdims=True))
        found.append(jnp.zeros((8 - q, LANES), F32))
        answers[origin] = jnp.concatenate(found, axis=0)
        return carry

    lax.fori_loop(0, places, look, 0)
    exchange(answers, returned, a2a_sem.at[1])
    returned[place] = answers[place]
    exchange_wait(answers, returned, a2a_sem.at[1])
    first, second = halves(returned[...].reshape(places * 8, LANES))
    lookup = jnp.concatenate([first, second], axis=0).astype(BF16)
    answer_row = owner * 8 + lax.shift_right_logical(rank_ref[...], 7)
    answer_lane = lax.bitwise_and(rank_ref[...], 127)
    for r in range(chunks):
        got = dot_nn(lookup, one_hot(answer_lane[r : r + 1], LANES))
        value = got[: places * 8] + got[places * 8 :]
        hit = rows_iota(places * 8) == answer_row[r : r + 1]
        found = jnp.sum(jnp.where(hit, value, 0.0), axis=0, keepdims=True)
        residual_ref[r : r + 1, :] = depart_ref[r : r + 1, :] - found


def per_device(sizes, perturbations, diffusivity, sea_mask, obs_owner, obs_cell, obs_depart, obs_weight):
    lat_size, lon_size, mem_size = sizes
    members, tile_rows, tile_cols = perturbations.shape
    count = obs_cell.shape[0]
    places = lat_size * lon_size
    capacity = max(2, 2 * count // places)
    q = max(1, capacity // LANES)
    block_rows = 8
    while block_rows < 3 * q:
        block_rows *= 2
    rows = count // LANES
    ext = tile_rows + 2 * RIM
    quarter = tile_rows // mem_size
    divisor = members * mem_size - 1
    vmem = pltpu.VMEM
    dma = pltpu.SemaphoreType.DMA
    as_rows = lambda a: a.reshape(rows, LANES)
    member_rows = jnp.transpose(perturbations, (1, 0, 2)).astype(F32)
    increment, residual = pl.pallas_call(
        functools.partial(kernel, (lat_size, lon_size, mem_size, places, q, block_rows, divisor)),
        out_shape=(
            jax.ShapeDtypeStruct((tile_rows, tile_cols), F32),
            jax.ShapeDtypeStruct((rows, LANES), F32),
        ),
        in_specs=[pl.BlockSpec(memory_space=vmem)] * 7,
        out_specs=(pl.BlockSpec(memory_space=vmem),) * 2,
        scratch_shapes=[
            vmem((ext, 8, 512), F32),
            vmem((2, ext, 512), F32),
            vmem((ext, 512), F32),
            vmem((ext, 512), F32),
            vmem((ext, 8, 384), F32),
            vmem((ext, 8, 384), F32),
            vmem((ext, 8, 384), F32),
            vmem((ext, 8, 384), F32),
            vmem((places, block_rows, LANES), F32),
            vmem((places, block_rows, LANES), F32),
            vmem((2, tile_rows, tile_cols), F32),
            vmem((tile_rows, tile_cols), F32),
            vmem((mem_size, 2, quarter, tile_cols), F32),
            vmem((mem_size, quarter, tile_cols), F32),
            vmem((mem_size, quarter, tile_cols), F32),
            vmem((2, quarter, tile_cols), F32),
            vmem((places, 8, LANES), F32),
            vmem((places, 8, LANES), F32),
            vmem((rows, LANES), jnp.int32),
            vmem((8 * tile_rows, LANES), F32),
            vmem((2, ext, 384), F32),
        ] + [dma((8,))] * 8 + [dma((6, 2)), dma((2, 2))],
        compiler_params=pltpu.CompilerParams(
            collective_id=0, has_side_effects=True, vmem_limit_bytes=40 * 1024 * 1024
        ),
        name="update",
    )(
        member_rows, diffusivity, sea_mask,
        as_rows(obs_owner), as_rows(obs_cell), as_rows(obs_depart), as_rows(obs_weight),
    )
    return increment, residual.reshape(count)


def solution(mesh):
    sizes = tuple(mesh.shape[name] for name in ("lat", "lon", "mem"))
    return jax.shard_map(
        functools.partial(per_device, sizes),
        mesh=mesh,
        in_specs=(
            P("mem", "lat", "lon"),
            P("lat", "lon"),
            P("lat", "lon"),
            P(("lat", "lon", "mem"), None),
            P(("lat", "lon", "mem")),
            P(("lat", "lon", "mem")),
            P(("lat", "lon", "mem")),
        ),
        out_specs=(P("lat", "lon"), P(("lat", "lon", "mem"))),
        check_vma=False,
    )
```

```python
import functools

import jax
import jax.numpy as jnp
from jax import lax
from jax.experimental import pallas as pl
from jax.experimental.pallas import tpu as pltpu
from jax.sharding import PartitionSpec as P

STEPS = 4
LANES = 128
RIM = 8
F32 = jnp.float32
BF16 = jnp.bfloat16
MESH = pl.DeviceIdType.MESH
DIRECTIONS = [(0, 1), (0, -1), (1, 0), (-1, 0), (1, 1), (1, -1), (-1, 1), (-1, -1)]


def halves(value):
    high = value.astype(BF16).astype(F32)
    return high, value - high


def dot_nt(left, right):
    return lax.dot_general(left, right, (((1,), (1,)), ((), ())), preferred_element_type=F32)


def dot_nn(left, right):
    return lax.dot_general(left, right, (((1,), (0,)), ((), ())), preferred_element_type=F32)


def rows_iota(count):
    return lax.broadcasted_iota(jnp.int32, (count, LANES), 0)


def one_hot(index_row, count):
    return jnp.where(rows_iota(count) == index_row, 1.0, 0.0).astype(BF16)


def kernel(
    sizes,
    member_ref, rate_ref, sea_ref, owner_ref, cell_ref, depart_ref, weight_ref,
    increment_ref, residual_ref,
    member_ext, coef_ext, source1, source2, spread, member_all, north_all, east_all,
    outgoing, arrived, partial1, partial, gathered1, gathered2, gathered3, kept, answers, returned,
    rank_ref, total_ref, wide_ref, lane_hot, column_hot,
    send_x, recv_x, send_c, recv_c, send_v1, recv_v1, send_v2, recv_v2, sums_sem, a2a_sem,
):
    lat_size, lon_size, mem_size, places, q, block_rows, divisor = sizes
    tile_rows, tile_cols = rate_ref.shape
    chunks = owner_ref.shape[0]
    lat = lax.axis_index("lat")
    lon = lax.axis_index("lon")
    mem = lax.axis_index("mem")
    place = lat * lon_size + lon
    quarter = tile_rows // mem_size
    shift_q = q.bit_length() - 1
    shift_b = block_rows.bit_length() - 1
    end = RIM + tile_rows
    ext_rows = tile_rows + 2 * RIM

    def place_at(step):
        other = lax.rem(place + step, places)
        return other, (other // lon_size, lax.rem(other, lon_size), mem)

    barrier = pltpu.get_barrier_semaphore()

    def greet(step, carry):
        pl.semaphore_signal(barrier, inc=1, device_id=place_at(step)[1], device_id_type=MESH)
        return carry

    lax.fori_loop(1, places, greet, 0)
    for step in range(1, mem_size):
        pl.semaphore_signal(
            barrier, inc=1, device_id=(lat, lon, lax.rem(mem + step, mem_size)), device_id_type=MESH
        )

    zero_rows = jnp.zeros((RIM, 512), F32)
    for ext in (source1, source2, coef_ext.at[0], coef_ext.at[1]):
        @pl.when(lat == 0)
        def _(ext=ext):
            ext[0:RIM, :] = zero_rows

        @pl.when(lat == lat_size - 1)
        def _(ext=ext):
            ext[end:ext_rows, :] = zero_rows

    @pl.when(lat == 0)
    def _():
        member_ext[0:RIM] = jnp.zeros((RIM, 8, 512), F32)

    @pl.when(lat == lat_size - 1)
    def _():
        member_ext[end:ext_rows] = jnp.zeros((RIM, 8, 512), F32)

    member_ext[RIM:end, :, 0:tile_cols] = member_ref[...]
    coef_ext[0, RIM:end, 0:tile_cols] = rate_ref[...]
    coef_ext[1, RIM:end, 0:tile_cols] = sea_ref[...].astype(F32)

    pl.semaphore_wait(barrier, places - 1 + mem_size - 1)

    def halo_copies(at, send_sem, recv_sem):
        made = []
        for k, (dy, dx) in enumerate(DIRECTIONS):
            source_rows = {0: pl.ds(RIM, tile_rows), 1: pl.ds(end - RIM, RIM), -1: pl.ds(RIM, RIM)}[dy]
            target_rows = {0: pl.ds(RIM, tile_rows), 1: pl.ds(0, RIM), -1: pl.ds(end, RIM)}[dy]
            source_cols = {0: pl.ds(0, 256), 1: pl.ds(128, 128), -1: pl.ds(0, 128)}[dx]
            target_cols = {0: pl.ds(0, 256), 1: pl.ds(384, 128), -1: pl.ds(256, 128)}[dx]
            copy = pltpu.make_async_remote_copy(
                src_ref=at(source_rows, source_cols),
                dst_ref=at(target_rows, target_cols),
                send_sem=send_sem.at[k],
                recv_sem=recv_sem.at[k],
                device_id=(lat + dy, lax.rem(lon + dx + lon_size, lon_size), mem),
                device_id_type=MESH,
            )
            sends = {0: None, 1: lat < lat_size - 1, -1: lat > 0}[dy]
            gets = {0: None, 1: lat > 0, -1: lat < lat_size - 1}[dy]
            made.append((copy, sends, gets))
        return made

    def when(condition, action):
        if condition is None:
            action()
        else:
            pl.when(condition)(action)

    def halo_start(copies):
        for copy, sends, gets in copies:
            when(sends, lambda copy=copy: copy.start())

    def halo_wait(copies):
        for copy, sends, gets in copies:
            when(sends, lambda copy=copy: copy.wait_send())
            when(gets, lambda copy=copy: copy.wait_recv())

    coef_copies = halo_copies(lambda r, c: coef_ext.at[:, r, c], send_c, recv_c)
    member_copies = halo_copies(lambda r, c: member_ext.at[r, :, c], send_x, recv_x)
    source_copies = [
        halo_copies(lambda r, c: source1.at[r, c], send_v1, recv_v1),
        halo_copies(lambda r, c: source2.at[r, c], send_v2, recv_v2),
    ]

    owner = owner_ref[...]
    upper = jnp.where(
        lax.broadcasted_iota(jnp.int32, (LANES, LANES), 0)
        < lax.broadcasted_iota(jnp.int32, (LANES, LANES), 1), 1.0, 0.0,
    ).astype(BF16)
    table = jnp.concatenate([upper, jnp.ones((LANES, LANES), BF16)], axis=1)
    before = jnp.zeros((places, LANES), F32)
    match = jnp.concatenate(
        [jnp.where(rows_iota(places) == owner[r : r + 1], 1.0, 0.0) for r in range(chunks)], axis=0
    )
    counts = dot_nn(match.astype(BF16), table)
    for r in range(chunks):
        part = slice(r * places, (r + 1) * places)
        found = jnp.sum(match[part] * (counts[part, :LANES] + before), axis=0, keepdims=True)
        rank_ref[r : r + 1, :] = found.astype(jnp.int32)
        before = before + counts[part, LANES:]
    rank = rank_ref[...]
    slot_row = owner * block_rows + lax.shift_right_logical(rank, 7)
    slot_lane = lax.bitwise_and(rank, 127)

    depart = depart_ref[...]
    weight = weight_ref[...]
    cell = cell_ref[...]
    product1, product2 = halves(weight * depart)
    weight1, weight2 = halves(weight)
    cell2 = lax.bitwise_and(cell, 127)
    cell1 = (cell - cell2).astype(F32)
    cell2 = cell2.astype(F32)
    pack_rows = places * block_rows
    row = rows_iota(pack_rows)
    inner = lax.bitwise_and(row, block_rows - 1)
    field = lax.shift_right_logical(inner, shift_q)
    base_row = row - lax.shift_left(field, shift_q)
    packed = jnp.zeros((2 * pack_rows, LANES), F32)
    for r in range(0, chunks, 4):
        lefts = []
        for c in range(r, r + 4):
            s = slice(c, c + 1)
            hit = base_row == slot_row[s]
            parts = [
                jnp.where(field == 0, of_product[s], jnp.where(field == 1, of_weight[s], of_cell[s]))
                for of_product, of_weight, of_cell in ((product1, weight1, cell1), (product2, weight2, cell2))
            ]
            lefts.append(jnp.concatenate([jnp.where(hit, p, 0.0) for p in parts], axis=0).astype(BF16))
            lane_hot[:, c * LANES : (c + 1) * LANES] = one_hot(slot_lane[s], LANES)
        right = lane_hot[:, r * LANES : (r + 4) * LANES]
        packed = packed + dot_nt(jnp.concatenate(lefts, axis=1), right)
    packed = packed[:pack_rows] + packed[pack_rows:]
    outgoing[...] = packed.reshape(places, block_rows, LANES)

    def exchange(from_ref, to_ref, sems):
        def send(step, carry):
            other, device = place_at(step)
            pltpu.make_async_remote_copy(
                src_ref=from_ref.at[other], dst_ref=to_ref.at[place],
                send_sem=sems.at[0], recv_sem=sems.at[1],
                device_id=device, device_id_type=MESH,
            ).start()
            return carry

        lax.fori_loop(1, places, send, 0)

    def exchange_wait(from_ref, to_ref, sems):
        whole = pltpu.make_async_remote_copy(
            src_ref=from_ref.at[pl.ds(0, places - 1)], dst_ref=to_ref.at[pl.ds(0, places - 1)],
            send_sem=sems.at[0], recv_sem=sems.at[1],
            device_id=place_at(1)[1], device_id_type=MESH,
        )
        whole.wait_send()
        whole.wait_recv()

    exchange(outgoing, arrived, a2a_sem.at[0])
    halo_start(coef_copies)
    halo_start(member_copies)
    arrived[place] = outgoing[place]
    exchange_wait(outgoing, arrived, a2a_sem.at[0])

    def slot_cells(block):
        whole = block[2 * q : 3 * q].astype(jnp.int32)
        return lax.shift_right_logical(whole, 8), lax.bitwise_and(whole, 255)

    total_ref[...] = jnp.zeros_like(total_ref)
    group = 2

    def add_blocks(step, carry):
        for u in range(group):
            origin = step * group + u
            block = arrived[origin]
            high, low = slot_cells(block)
            lefts = []
            for k in range(q):
                hit = rows_iota(tile_rows) == high[k : k + 1]
                parts = halves(block[k : k + 1]) + halves(block[q + k : q + k + 1])
                lefts.append(jnp.concatenate([jnp.where(hit, p, 0.0) for p in parts], axis=0).astype(BF16))
                column_hot[origin, :, k * LANES : (k + 1) * LANES] = one_hot(low[k : k + 1], tile_cols)
            total_ref[...] += dot_nt(jnp.concatenate(lefts, axis=1), column_hot[origin])
        return carry

    lax.fori_loop(0, places // group, add_blocks, 0)
    for f in range(2):
        start = 2 * f * tile_rows
        partial1[f] = total_ref[start : start + tile_rows, :] + total_ref[start + tile_rows : start + 2 * tile_rows, :]

    my_rows = pl.multiple_of(mem * quarter, quarter)

    def sum_copy(part_at, got, number, other):
        sems = sums_sem.at[2 * number]
        return pltpu.make_async_remote_copy(
            src_ref=part_at(pl.ds(pl.multiple_of(other * quarter, quarter), quarter)),
            dst_ref=got.at[mem],
            send_sem=sems.at[0], recv_sem=sems.at[1],
            device_id=(lat, lon, other), device_id_type=MESH,
        )

    def sum_part(part_at, got, number, other):
        @pl.when(mem != other)
        def _():
            sum_copy(part_at, got, number, other).start()

    def member_sum(part_at, got, number):
        sems = sums_sem.at[2 * number]
        got[mem] = part_at(pl.ds(my_rows, quarter))[...]
        whole = pltpu.make_async_remote_copy(
            src_ref=got.at[pl.ds(0, mem_size - 1)], dst_ref=got.at[pl.ds(0, mem_size - 1)],
            send_sem=sems.at[0], recv_sem=sems.at[1],
            device_id=(lat, lon, lax.rem(mem + 1, mem_size)), device_id_type=MESH,
        )
        whole.wait_send()
        whole.wait_recv()
        total = got[0]
        for other in range(1, mem_size):
            total = total + got[other]
        return total

    def member_share(ref, first, number):
        sems = sums_sem.at[2 * number + 1]
        mine = ref.at[pl.ds(first + my_rows, quarter), pl.ds(0, tile_cols)]
        for step in range(1, mem_size):
            pltpu.make_async_remote_copy(
                src_ref=mine, dst_ref=mine,
                send_sem=sems.at[0], recv_sem=sems.at[1],
                device_id=(lat, lon, lax.rem(mem + step, mem_size)), device_id_type=MESH,
            ).start()
        rest = ref.at[pl.ds(first, (mem_size - 1) * quarter), pl.ds(0, tile_cols)]
        whole = pltpu.make_async_remote_copy(
            src_ref=rest, dst_ref=rest, send_sem=sems.at[0], recv_sem=sems.at[1],
            device_id=(lat, lon, lax.rem(mem + 1, mem_size)), device_id_type=MESH,
        )
        whole.wait_send()
        whole.wait_recv()

    first_part = lambda rows: partial1.at[:, rows]
    for step in range(1, mem_size):
        sum_copy(first_part, gathered1, 0, lax.rem(mem + step, mem_size)).start()
    summed = member_sum(first_part, gathered1, 0)
    kept[...] = summed
    source1[pl.ds(RIM + my_rows, quarter), 0:tile_cols] = summed[0]
    member_share(source1, RIM, 0)
    halo_start(source_copies[0])

    lane = lax.broadcasted_iota(jnp.int32, (1, LANES), 1)

    def joined(value):
        side = jnp.where(lane < 64, value[..., 256:384], value[..., 384:512])
        return jnp.concatenate([value[..., 0:256], side], axis=-1)

    halo_wait(coef_copies)
    halo_wait(member_copies)
    rate = joined(coef_ext[0])
    sea = joined(coef_ext[1])
    below = lambda a: jnp.concatenate([a[1:], a[:1]], axis=0)
    width = 384
    wide_ref[0] = 0.5 * (rate + below(rate)) * sea * below(sea)
    wide_ref[1] = 0.5 * (rate + pltpu.roll(rate, width - 1, 1)) * sea * pltpu.roll(sea, width - 1, 1)

    def widen(step, carry):
        base = pl.multiple_of(step * 8, 8)
        for u in range(8):
            i = base + u
            north_all[i] = jnp.broadcast_to(wide_ref[0, pl.ds(i, 1), :], (8, width))
            east_all[i] = jnp.broadcast_to(wide_ref[1, pl.ds(i, 1), :], (8, width))
            value = member_ext[i]
            side = jnp.where(lane < 64, value[:, 256:384], value[:, 384:512])
            member_all[i, :, 0:256] = value[:, 0:256]
            member_all[i, :, 256:384] = side
        return carry

    lax.fori_loop(0, ext_rows // 8, widen, 0)

    def covariance(source, finished):
        wide_ref[0] = joined(source[...])

        def step_rows(read, base, carry, count):
            here, flux = carry
            values = [here] + [read(base + u + 1) for u in range(count)]
            results = []
            for u in range(count):
                here, after = values[u], values[u + 1]
                flux_after = north_all[base + u] * (after - here)
                flux_east = east_all[base + u] * (pltpu.roll(here, width - 1, 1) - here)
                results.append(here + (flux_after - flux) + (flux_east - pltpu.roll(flux_east, 1, 1)))
                flux = flux_after
            return results, (values[-1], flux)

        def first_of(read, row):
            here = read(row)
            return here, north_all[row - 1] * (here - read(row - 1))

        def sweep(read):
            def rows(step, carry):
                base = 4 + step * 8
                results, carry = step_rows(read, base, carry, 8)
                for u in range(8):
                    spread[base + u] = results[u]
                return carry

            lax.fori_loop(0, (tile_rows + 8) // 8, rows, first_of(read, 4))

        def begin(i):
            return member_all[i] * wide_ref[0, pl.ds(i, 1), :]

        def again(i):
            return spread[i]

        spread[3] = begin(3)
        spread[tile_rows + 12] = begin(tile_rows + 12)
        sweep(begin)
        for turn in range(STEPS - 2):
            sweep(again)

        def last_rows(step, carry):
            base = RIM + step * 8
            results, carry = step_rows(again, base, carry, 8)
            found = [
                jnp.sum(results[u][:, 0:256] * member_all[base + u, :, 0:256], axis=0, keepdims=True)
                for u in range(8)
            ]
            partial[pl.ds(pl.multiple_of(step * 8, 8), 8), :] = jnp.concatenate(found, axis=0)
            return carry

        carry = first_of(again, RIM)
        steps = quarter // 8
        for part in range(mem_size):
            carry = lax.fori_loop(part * steps, (part + 1) * steps, last_rows, carry)
            finished(part)

    my_sea = lambda: coef_ext[1, pl.ds(RIM + my_rows, quarter), 0:tile_cols]
    halo_wait(source_copies[0])
    later_part = lambda rows: partial.at[rows]
    covariance(source1, lambda part: sum_part(later_part, gathered2, 1, part))
    first_pass = my_sea() * member_sum(later_part, gathered2, 1) / divisor
    source2[pl.ds(RIM + my_rows, quarter), 0:tile_cols] = kept[0] - kept[1] * first_pass
    member_share(source2, RIM, 1)
    halo_start(source_copies[1])
    halo_wait(source_copies[1])
    covariance(source2, lambda part: sum_part(later_part, gathered3, 2, part))
    wide = my_sea() * member_sum(later_part, gathered3, 2) / divisor
    increment_ref[pl.ds(my_rows, quarter), :] = wide
    member_share(increment_ref, 0, 2)

    first, second = halves(increment_ref[...])
    lookup = jnp.concatenate([first, second], axis=0).astype(BF16)

    def look(step, carry):
        for u in range(group):
            origin = step * group + u
            high, low = slot_cells(arrived[origin])
            got = dot_nn(lookup, column_hot[origin])
            value = got[:tile_rows] + got[tile_rows:]
            found = []
            for k in range(q):
                hit = rows_iota(tile_rows) == high[k : k + 1]
                part = value[:, k * LANES : (k + 1) * LANES]
                found.append(jnp.sum(jnp.where(hit, part, 0.0), axis=0, keepdims=True))
            found.append(jnp.zeros((8 - q, LANES), F32))
            answers[origin] = jnp.concatenate(found, axis=0)
        return carry

    lax.fori_loop(0, places // group, look, 0)
    exchange(answers, returned, a2a_sem.at[1])
    returned[place] = answers[place]
    exchange_wait(answers, returned, a2a_sem.at[1])
    first, second = halves(returned[...].reshape(places * 8, LANES))
    lookup = jnp.concatenate([first, second], axis=0).astype(BF16)
    answer_row = owner * 8 + lax.shift_right_logical(rank_ref[...], 7)
    got = dot_nn(lookup, lane_hot[...])
    values = got[: places * 8] + got[places * 8 :]
    for r in range(chunks):
        value = values[:, r * LANES : (r + 1) * LANES]
        hit = rows_iota(places * 8) == answer_row[r : r + 1]
        found = jnp.sum(jnp.where(hit, value, 0.0), axis=0, keepdims=True)
        residual_ref[r : r + 1, :] = depart_ref[r : r + 1, :] - found


def per_device(sizes, perturbations, diffusivity, sea_mask, obs_owner, obs_cell, obs_depart, obs_weight):
    lat_size, lon_size, mem_size = sizes
    members, tile_rows, tile_cols = perturbations.shape
    count = obs_cell.shape[0]
    places = lat_size * lon_size
    capacity = max(2, 2 * count // places)
    q = max(1, capacity // LANES)
    block_rows = 8
    while block_rows < 3 * q:
        block_rows *= 2
    rows = count // LANES
    ext = tile_rows + 2 * RIM
    quarter = tile_rows // mem_size
    divisor = members * mem_size - 1
    vmem = pltpu.VMEM
    dma = pltpu.SemaphoreType.DMA
    as_rows = lambda a: a.reshape(rows, LANES)
    member_rows = jnp.transpose(perturbations, (1, 0, 2)).astype(F32)
    increment, residual = pl.pallas_call(
        functools.partial(kernel, (lat_size, lon_size, mem_size, places, q, block_rows, divisor)),
        out_shape=(
            jax.ShapeDtypeStruct((tile_rows, tile_cols), F32),
            jax.ShapeDtypeStruct((rows, LANES), F32),
        ),
        in_specs=[pl.BlockSpec(memory_space=vmem)] * 7,
        out_specs=(pl.BlockSpec(memory_space=vmem),) * 2,
        scratch_shapes=[
            vmem((ext, 8, 512), F32),
            vmem((2, ext, 512), F32),
            vmem((ext, 512), F32),
            vmem((ext, 512), F32),
            vmem((ext, 8, 384), F32),
            vmem((ext, 8, 384), F32),
            vmem((ext, 8, 384), F32),
            vmem((ext, 8, 384), F32),
            vmem((places, block_rows, LANES), F32),
            vmem((places, block_rows, LANES), F32),
            vmem((2, tile_rows, tile_cols), F32),
            vmem((tile_rows, tile_cols), F32),
            vmem((mem_size, 2, quarter, tile_cols), F32),
            vmem((mem_size, quarter, tile_cols), F32),
            vmem((mem_size, quarter, tile_cols), F32),
            vmem((2, quarter, tile_cols), F32),
            vmem((places, 8, LANES), F32),
            vmem((places, 8, LANES), F32),
            vmem((rows, LANES), jnp.int32),
            vmem((4 * tile_rows, tile_cols), F32),
            vmem((2, ext, 384), F32),
            vmem((LANES, count), BF16),
            vmem((places, tile_cols, q * LANES), BF16),
        ] + [dma((8,))] * 8 + [dma((6, 2)), dma((2, 2))],
        compiler_params=pltpu.CompilerParams(
            collective_id=0, has_side_effects=True, vmem_limit_bytes=40 * 1024 * 1024
        ),
        name="update",
    )(
        member_rows, diffusivity, sea_mask,
        as_rows(obs_owner), as_rows(obs_cell), as_rows(obs_depart), as_rows(obs_weight),
    )
    return increment, residual.reshape(count)


def solution(mesh):
    sizes = tuple(mesh.shape[name] for name in ("lat", "lon", "mem"))
    return jax.shard_map(
        functools.partial(per_device, sizes),
        mesh=mesh,
        in_specs=(
            P("mem", "lat", "lon"),
            P("lat", "lon"),
            P("lat", "lon"),
            P(("lat", "lon", "mem"), None),
            P(("lat", "lon", "mem")),
            P(("lat", "lon", "mem")),
            P(("lat", "lon", "mem")),
        ),
        out_specs=(P("lat", "lon"), P(("lat", "lon", "mem"))),
        check_vma=False,
    )
```

```python
import functools

import jax
import jax.numpy as jnp
from jax import lax
from jax.experimental import pallas as pl
from jax.experimental.pallas import tpu as pltpu
from jax.sharding import PartitionSpec as P

STEPS = 4
LANES = 128
RIM = 8
F32 = jnp.float32
BF16 = jnp.bfloat16
MESH = pl.DeviceIdType.MESH
DIRECTIONS = [(0, 1), (0, -1), (1, 0), (-1, 0), (1, 1), (1, -1), (-1, 1), (-1, -1)]
EVERY = range(8)
SIDES = (0, 1, 4, 5, 6, 7)
AHEAD = (2, 3)
WIDE = {0: (pl.ds(0, 256), pl.ds(0, 256)), 1: (pl.ds(128, 128), pl.ds(384, 128)), -1: (pl.ds(0, 128), pl.ds(256, 128))}
NARROW = {1: (pl.ds(0, 128), pl.ds(256, 128)), -1: (pl.ds(0, 128), pl.ds(128, 128))}


def halves(value):
    high = value.astype(BF16).astype(F32)
    return high, value - high


def dot_nt(left, right):
    return lax.dot_general(left, right, (((1,), (1,)), ((), ())), preferred_element_type=F32)


def dot_nn(left, right):
    return lax.dot_general(left, right, (((1,), (0,)), ((), ())), preferred_element_type=F32)


def rows_iota(count):
    return lax.broadcasted_iota(jnp.int32, (count, LANES), 0)


def one_hot(index_row, count):
    return jnp.where(rows_iota(count) == index_row, 1.0, 0.0).astype(BF16)


def kernel(
    sizes,
    member_ref, plain_ref, rate_ref, sea_ref, owner_ref, cell_ref, depart_ref, weight_ref,
    increment_ref, residual_ref,
    member_all, edge_ext, coef_ext, source1, source2, spread, north_all, east_all,
    outgoing, arrived, partial1, partial, gathered1, gathered2, gathered3, kept, answers, returned,
    rank_ref, total_ref, wide_ref, lane_hot, column_hot,
    send_x, recv_x, send_e, recv_e, send_c, recv_c, send_v1, recv_v1, send_v2, recv_v2, sums_sem, a2a_sem,
):
    lat_size, lon_size, mem_size, places, q, block_rows, divisor = sizes
    tile_rows, tile_cols = rate_ref.shape
    chunks = owner_ref.shape[0]
    lat = lax.axis_index("lat")
    lon = lax.axis_index("lon")
    mem = lax.axis_index("mem")
    place = lat * lon_size + lon
    quarter = tile_rows // mem_size
    shift_q = q.bit_length() - 1
    shift_b = block_rows.bit_length() - 1
    end = RIM + tile_rows
    ext_rows = tile_rows + 2 * RIM

    def place_at(step):
        other = lax.rem(place + step, places)
        return other, (other // lon_size, lax.rem(other, lon_size), mem)

    barrier = pltpu.get_barrier_semaphore()

    def greet(step, carry):
        pl.semaphore_signal(barrier, inc=1, device_id=place_at(step)[1], device_id_type=MESH)
        return carry

    lax.fori_loop(1, places, greet, 0)
    for step in range(1, mem_size):
        pl.semaphore_signal(
            barrier, inc=1, device_id=(lat, lon, lax.rem(mem + step, mem_size)), device_id_type=MESH
        )

    zero_rows = jnp.zeros((RIM, 512), F32)
    for ext in (source1, source2, coef_ext.at[0], coef_ext.at[1]):
        @pl.when(lat == 0)
        def _(ext=ext):
            ext[0:RIM, :] = zero_rows

        @pl.when(lat == lat_size - 1)
        def _(ext=ext):
            ext[end:ext_rows, :] = zero_rows

    @pl.when(lat == 0)
    def _():
        member_all[0:RIM] = jnp.zeros((RIM, 8, 384), F32)
        edge_ext[0:RIM] = jnp.zeros((RIM, 3 * LANES), F32)

    @pl.when(lat == lat_size - 1)
    def _():
        member_all[end:ext_rows] = jnp.zeros((RIM, 8, 384), F32)
        edge_ext[end:ext_rows] = jnp.zeros((RIM, 3 * LANES), F32)

    member_all[0:4, :, 0:tile_cols] = jnp.zeros((4, 8, tile_cols), F32)
    member_all[end + 4 : ext_rows, :, 0:tile_cols] = jnp.zeros((4, 8, tile_cols), F32)
    member_all[RIM:end, :, 0:tile_cols] = member_ref[...]
    lane = lax.broadcasted_iota(jnp.int32, (1, LANES), 1)
    edges = jnp.zeros((tile_rows, LANES), F32)
    for m in range(8):
        middle = 8 * (8 - m)
        first_cols = plain_ref[m, :, 0:LANES].astype(F32)
        last_cols = plain_ref[m, :, tile_cols - LANES : tile_cols].astype(F32)
        turned = pltpu.roll(jnp.where(lane < 64, first_cols, last_cols), middle, 1)
        edges = jnp.where((lane >= middle - 4) & (lane < middle + 4), turned, edges)
    edge_ext[RIM:end, 0:LANES] = edges
    coef_ext[0, RIM:end, 0:tile_cols] = rate_ref[...]
    coef_ext[1, RIM:end, 0:tile_cols] = sea_ref[...].astype(F32)

    pl.semaphore_wait(barrier, places - 1 + mem_size - 1)

    def halo_copies(at, send_sem, recv_sem, directions, depth=RIM, cols=None):
        made = []
        for k in directions:
            dy, dx = DIRECTIONS[k]
            source_rows = {0: pl.ds(RIM, tile_rows), 1: pl.ds(end - depth, depth), -1: pl.ds(RIM, depth)}[dy]
            target_rows = {0: pl.ds(RIM, tile_rows), 1: pl.ds(RIM - depth, depth), -1: pl.ds(end, depth)}[dy]
            source_cols, target_cols = (cols or WIDE)[dx]
            copy = pltpu.make_async_remote_copy(
                src_ref=at(source_rows, source_cols),
                dst_ref=at(target_rows, target_cols),
                send_sem=send_sem.at[k],
                recv_sem=recv_sem.at[k],
                device_id=(lat + dy, lax.rem(lon + dx + lon_size, lon_size), mem),
                device_id_type=MESH,
            )
            sends = {0: None, 1: lat < lat_size - 1, -1: lat > 0}[dy]
            gets = {0: None, 1: lat > 0, -1: lat < lat_size - 1}[dy]
            made.append((copy, sends, gets))
        return made

    def when(condition, action):
        if condition is None:
            action()
        else:
            pl.when(condition)(action)

    def halo_start(copies):
        for copy, sends, gets in copies:
            when(sends, lambda copy=copy: copy.start())

    sent = []

    def halo_wait(copies):
        for copy, sends, gets in copies:
            when(gets, lambda copy=copy: copy.wait_recv())
            sent.append(lambda copy=copy, sends=sends: when(sends, lambda: copy.wait_send()))

    coef_copies = halo_copies(lambda r, c: coef_ext.at[:, r, c], send_c, recv_c, EVERY)
    edge_copies = halo_copies(lambda r, c: edge_ext.at[r, c], send_e, recv_e, SIDES, cols=NARROW)
    member_copies = halo_copies(lambda r, c: member_all.at[r, :, c], send_x, recv_x, AHEAD, depth=4)
    source_copies = [
        halo_copies(lambda r, c: source1.at[r, c], send_v1, recv_v1, EVERY),
        halo_copies(lambda r, c: source2.at[r, c], send_v2, recv_v2, EVERY),
    ]

    owner = owner_ref[...]
    upper = jnp.where(
        lax.broadcasted_iota(jnp.int32, (LANES, LANES), 0)
        < lax.broadcasted_iota(jnp.int32, (LANES, LANES), 1), 1.0, 0.0,
    ).astype(BF16)
    table = jnp.concatenate([upper, jnp.ones((LANES, LANES), BF16)], axis=1)
    before = jnp.zeros((places, LANES), F32)
    match = jnp.concatenate(
        [jnp.where(rows_iota(places) == owner[r : r + 1], 1.0, 0.0) for r in range(chunks)], axis=0
    )
    counts = dot_nn(match.astype(BF16), table)
    for r in range(chunks):
        part = slice(r * places, (r + 1) * places)
        found = jnp.sum(match[part] * (counts[part, :LANES] + before), axis=0, keepdims=True)
        rank_ref[r : r + 1, :] = found.astype(jnp.int32)
        before = before + counts[part, LANES:]
    rank = rank_ref[...]
    slot_row = owner * block_rows + lax.shift_right_logical(rank, 7)
    slot_lane = lax.bitwise_and(rank, 127)

    depart = depart_ref[...]
    weight = weight_ref[...]
    cell = cell_ref[...]
    product1, product2 = halves(weight * depart)
    weight1, weight2 = halves(weight)
    cell2 = lax.bitwise_and(cell, 127)
    cell1 = (cell - cell2).astype(F32)
    cell2 = cell2.astype(F32)
    pack_rows = places * block_rows
    row = rows_iota(pack_rows)
    inner = lax.bitwise_and(row, block_rows - 1)
    field = lax.shift_right_logical(inner, shift_q)
    base_row = row - lax.shift_left(field, shift_q)
    packed = jnp.zeros((2 * pack_rows, LANES), F32)
    for r in range(0, chunks, 4):
        lefts = []
        for c in range(r, r + 4):
            s = slice(c, c + 1)
            hit = base_row == slot_row[s]
            parts = [
                jnp.where(field == 0, of_product[s], jnp.where(field == 1, of_weight[s], of_cell[s]))
                for of_product, of_weight, of_cell in ((product1, weight1, cell1), (product2, weight2, cell2))
            ]
            lefts.append(jnp.concatenate([jnp.where(hit, p, 0.0) for p in parts], axis=0).astype(BF16))
            lane_hot[:, c * LANES : (c + 1) * LANES] = one_hot(slot_lane[s], LANES)
        right = lane_hot[:, r * LANES : (r + 4) * LANES]
        packed = packed + dot_nt(jnp.concatenate(lefts, axis=1), right)
    packed = packed[:pack_rows] + packed[pack_rows:]
    outgoing[...] = packed.reshape(places, block_rows, LANES)

    def exchange(from_ref, to_ref, sems):
        def send(step, carry):
            other, device = place_at(step)
            pltpu.make_async_remote_copy(
                src_ref=from_ref.at[other], dst_ref=to_ref.at[place],
                send_sem=sems.at[0], recv_sem=sems.at[1],
                device_id=device, device_id_type=MESH,
            ).start()
            return carry

        lax.fori_loop(1, places, send, 0)

    def exchange_wait(from_ref, to_ref, sems):
        whole = pltpu.make_async_remote_copy(
            src_ref=from_ref.at[pl.ds(0, places - 1)], dst_ref=to_ref.at[pl.ds(0, places - 1)],
            send_sem=sems.at[0], recv_sem=sems.at[1],
            device_id=place_at(1)[1], device_id_type=MESH,
        )
        whole.wait_recv()
        sent.append(whole.wait_send)

    exchange(outgoing, arrived, a2a_sem.at[0])
    halo_start(coef_copies)
    halo_start(edge_copies)
    halo_start(member_copies)
    arrived[place] = outgoing[place]
    exchange_wait(outgoing, arrived, a2a_sem.at[0])

    def slot_cells(block):
        whole = block[2 * q : 3 * q].astype(jnp.int32)
        return lax.shift_right_logical(whole, 8), lax.bitwise_and(whole, 255)

    total_ref[...] = jnp.zeros_like(total_ref)
    group = 2

    def add_blocks(step, carry):
        for u in range(group):
            origin = step * group + u
            block = arrived[origin]
            high, low = slot_cells(block)
            lefts = []
            for k in range(q):
                hit = rows_iota(tile_rows) == high[k : k + 1]
                parts = halves(block[k : k + 1]) + halves(block[q + k : q + k + 1])
                lefts.append(jnp.concatenate([jnp.where(hit, p, 0.0) for p in parts], axis=0).astype(BF16))
                column_hot[origin, :, k * LANES : (k + 1) * LANES] = one_hot(low[k : k + 1], tile_cols)
            total_ref[...] += dot_nt(jnp.concatenate(lefts, axis=1), column_hot[origin])
        return carry

    lax.fori_loop(0, places // group, add_blocks, 0)
    for f in range(2):
        start = 2 * f * tile_rows
        partial1[f] = total_ref[start : start + tile_rows, :] + total_ref[start + tile_rows : start + 2 * tile_rows, :]

    my_rows = pl.multiple_of(mem * quarter, quarter)

    def sum_copy(part_at, got, number, other):
        sems = sums_sem.at[2 * number]
        return pltpu.make_async_remote_copy(
            src_ref=part_at(pl.ds(pl.multiple_of(other * quarter, quarter), quarter)),
            dst_ref=got.at[mem],
            send_sem=sems.at[0], recv_sem=sems.at[1],
            device_id=(lat, lon, other), device_id_type=MESH,
        )

    def sum_part(part_at, got, number, other):
        @pl.when(mem != other)
        def _():
            sum_copy(part_at, got, number, other).start()

    def member_sum(part_at, got, number):
        sems = sums_sem.at[2 * number]
        got[mem] = part_at(pl.ds(my_rows, quarter))[...]
        whole = pltpu.make_async_remote_copy(
            src_ref=got.at[pl.ds(0, mem_size - 1)], dst_ref=got.at[pl.ds(0, mem_size - 1)],
            send_sem=sems.at[0], recv_sem=sems.at[1],
            device_id=(lat, lon, lax.rem(mem + 1, mem_size)), device_id_type=MESH,
        )
        whole.wait_recv()
        sent.append(whole.wait_send)
        total = got[0]
        for other in range(1, mem_size):
            total = total + got[other]
        return total

    def member_share(ref, first, number):
        sems = sums_sem.at[2 * number + 1]
        mine = ref.at[pl.ds(first + my_rows, quarter), pl.ds(0, tile_cols)]
        for step in range(1, mem_size):
            pltpu.make_async_remote_copy(
                src_ref=mine, dst_ref=mine,
                send_sem=sems.at[0], recv_sem=sems.at[1],
                device_id=(lat, lon, lax.rem(mem + step, mem_size)), device_id_type=MESH,
            ).start()
        rest = ref.at[pl.ds(first, (mem_size - 1) * quarter), pl.ds(0, tile_cols)]
        whole = pltpu.make_async_remote_copy(
            src_ref=rest, dst_ref=rest, send_sem=sems.at[0], recv_sem=sems.at[1],
            device_id=(lat, lon, lax.rem(mem + 1, mem_size)), device_id_type=MESH,
        )
        whole.wait_recv()
        sent.append(whole.wait_send)

    first_part = lambda rows: partial1.at[:, rows]
    for step in range(1, mem_size):
        sum_copy(first_part, gathered1, 0, lax.rem(mem + step, mem_size)).start()
    summed = member_sum(first_part, gathered1, 0)
    kept[...] = summed
    source1[pl.ds(RIM + my_rows, quarter), 0:tile_cols] = summed[0]
    member_share(source1, RIM, 0)
    halo_start(source_copies[0])


    def joined(value):
        side = jnp.where(lane < 64, value[..., 256:384], value[..., 384:512])
        return jnp.concatenate([value[..., 0:256], side], axis=-1)

    halo_wait(coef_copies)
    halo_wait(edge_copies)
    halo_wait(member_copies)
    rate = joined(coef_ext[0])
    sea = joined(coef_ext[1])
    below = lambda a: jnp.concatenate([a[1:], a[:1]], axis=0)
    width = 384
    wide_ref[0] = 0.5 * (rate + below(rate)) * sea * below(sea)
    wide_ref[1] = 0.5 * (rate + pltpu.roll(rate, width - 1, 1)) * sea * pltpu.roll(sea, width - 1, 1)

    def widen(step, carry):
        base = pl.multiple_of(step * 8, 8)
        for u in range(8):
            i = base + u
            north_all[i] = jnp.broadcast_to(wide_ref[0, pl.ds(i, 1), :], (8, width))
            east_all[i] = jnp.broadcast_to(wide_ref[1, pl.ds(i, 1), :], (8, width))
            line = edge_ext[pl.ds(i, 1), :]
            both = jnp.where(lax.bitwise_and(lane, 7) < 4, line[:, 128:256], line[:, 256:384])
            member_all[i, :, 256:384] = pltpu.roll(
                jnp.broadcast_to(both, (8, LANES)), 64, 1, stride=8, stride_axis=0
            )
        return carry

    lax.fori_loop(0, ext_rows // 8, widen, 0)

    def covariance(source, finished):
        wide_ref[0] = joined(source[...])

        def step_rows(read, base, carry, count):
            here, flux = carry
            values = [here] + [read(base + u + 1) for u in range(count)]
            results = []
            for u in range(count):
                here, after = values[u], values[u + 1]
                flux_after = north_all[base + u] * (after - here)
                flux_east = east_all[base + u] * (pltpu.roll(here, width - 1, 1) - here)
                results.append(here + (flux_after - flux) + (flux_east - pltpu.roll(flux_east, 1, 1)))
                flux = flux_after
            return results, (values[-1], flux)

        def first_of(read, row):
            here = read(row)
            return here, north_all[row - 1] * (here - read(row - 1))

        def sweep(read):
            def rows(step, carry):
                base = 4 + step * 8
                results, carry = step_rows(read, base, carry, 8)
                for u in range(8):
                    spread[base + u] = results[u]
                return carry

            lax.fori_loop(0, (tile_rows + 8) // 8, rows, first_of(read, 4))

        def begin(i):
            return member_all[i] * wide_ref[0, pl.ds(i, 1), :]

        def again(i):
            return spread[i]

        spread[3] = begin(3)
        spread[tile_rows + 12] = begin(tile_rows + 12)
        sweep(begin)
        for turn in range(STEPS - 2):
            sweep(again)

        def last_rows(step, carry):
            base = RIM + step * 8
            results, carry = step_rows(again, base, carry, 8)
            found = [
                jnp.sum(results[u][:, 0:256] * member_all[base + u, :, 0:256], axis=0, keepdims=True)
                for u in range(8)
            ]
            partial[pl.ds(pl.multiple_of(step * 8, 8), 8), :] = jnp.concatenate(found, axis=0)
            return carry

        carry = first_of(again, RIM)
        steps = quarter // 8
        for part in range(mem_size):
            carry = lax.fori_loop(part * steps, (part + 1) * steps, last_rows, carry)
            finished(part)

    my_sea = lambda: coef_ext[1, pl.ds(RIM + my_rows, quarter), 0:tile_cols]
    halo_wait(source_copies[0])
    later_part = lambda rows: partial.at[rows]
    covariance(source1, lambda part: sum_part(later_part, gathered2, 1, part))
    first_total = member_sum(later_part, gathered2, 1)
    sum_sent = sent.pop()
    first_pass = my_sea() * first_total / divisor
    source2[pl.ds(RIM + my_rows, quarter), 0:tile_cols] = kept[0] - kept[1] * first_pass
    member_share(source2, RIM, 1)
    halo_start(source_copies[1])
    halo_wait(source_copies[1])
    sum_sent()
    covariance(source2, lambda part: sum_part(later_part, gathered3, 2, part))
    wide = my_sea() * member_sum(later_part, gathered3, 2) / divisor
    increment_ref[pl.ds(my_rows, quarter), :] = wide
    member_share(increment_ref, 0, 2)

    first, second = halves(increment_ref[...])
    lookup = jnp.concatenate([first, second], axis=0).astype(BF16)

    def look(step, carry):
        for u in range(group):
            origin = step * group + u
            high, low = slot_cells(arrived[origin])
            got = dot_nn(lookup, column_hot[origin])
            value = got[:tile_rows] + got[tile_rows:]
            found = []
            for k in range(q):
                hit = rows_iota(tile_rows) == high[k : k + 1]
                part = value[:, k * LANES : (k + 1) * LANES]
                found.append(jnp.sum(jnp.where(hit, part, 0.0), axis=0, keepdims=True))
            found.append(jnp.zeros((8 - q, LANES), F32))
            answers[origin] = jnp.concatenate(found, axis=0)
        return carry

    lax.fori_loop(0, places // group, look, 0)
    exchange(answers, returned, a2a_sem.at[1])
    returned[place] = answers[place]
    exchange_wait(answers, returned, a2a_sem.at[1])
    first, second = halves(returned[...].reshape(places * 8, LANES))
    lookup = jnp.concatenate([first, second], axis=0).astype(BF16)
    answer_row = owner * 8 + lax.shift_right_logical(rank_ref[...], 7)
    got = dot_nn(lookup, lane_hot[...])
    values = got[: places * 8] + got[places * 8 :]
    for r in range(chunks):
        value = values[:, r * LANES : (r + 1) * LANES]
        hit = rows_iota(places * 8) == answer_row[r : r + 1]
        found = jnp.sum(jnp.where(hit, value, 0.0), axis=0, keepdims=True)
        residual_ref[r : r + 1, :] = depart_ref[r : r + 1, :] - found
    for wait in sent:
        wait()


def per_device(sizes, perturbations, diffusivity, sea_mask, obs_owner, obs_cell, obs_depart, obs_weight):
    lat_size, lon_size, mem_size = sizes
    members, tile_rows, tile_cols = perturbations.shape
    count = obs_cell.shape[0]
    places = lat_size * lon_size
    capacity = max(2, 2 * count // places)
    q = max(1, capacity // LANES)
    block_rows = 8
    while block_rows < 3 * q:
        block_rows *= 2
    rows = count // LANES
    ext = tile_rows + 2 * RIM
    quarter = tile_rows // mem_size
    divisor = members * mem_size - 1
    vmem = pltpu.VMEM
    dma = pltpu.SemaphoreType.DMA
    as_rows = lambda a: a.reshape(rows, LANES)
    member_rows = jnp.transpose(perturbations, (1, 0, 2)).astype(F32)
    increment, residual = pl.pallas_call(
        functools.partial(kernel, (lat_size, lon_size, mem_size, places, q, block_rows, divisor)),
        out_shape=(
            jax.ShapeDtypeStruct((tile_rows, tile_cols), F32),
            jax.ShapeDtypeStruct((rows, LANES), F32),
        ),
        in_specs=[pl.BlockSpec(memory_space=vmem)] * 8,
        out_specs=(pl.BlockSpec(memory_space=vmem),) * 2,
        scratch_shapes=[
            vmem((ext, 8, 384), F32),
            vmem((ext, 3 * LANES), F32),
            vmem((2, ext, 512), F32),
            vmem((ext, 512), F32),
            vmem((ext, 512), F32),
            vmem((ext, 8, 384), F32),
            vmem((ext, 8, 384), F32),
            vmem((ext, 8, 384), F32),
            vmem((places, block_rows, LANES), F32),
            vmem((places, block_rows, LANES), F32),
            vmem((2, tile_rows, tile_cols), F32),
            vmem((tile_rows, tile_cols), F32),
            vmem((mem_size, 2, quarter, tile_cols), F32),
            vmem((mem_size, quarter, tile_cols), F32),
            vmem((mem_size, quarter, tile_cols), F32),
            vmem((2, quarter, tile_cols), F32),
            vmem((places, 8, LANES), F32),
            vmem((places, 8, LANES), F32),
            vmem((rows, LANES), jnp.int32),
            vmem((4 * tile_rows, tile_cols), F32),
            vmem((2, ext, 384), F32),
            vmem((LANES, count), BF16),
            vmem((places, tile_cols, q * LANES), BF16),
        ] + [dma((8,))] * 10 + [dma((6, 2)), dma((2, 2))],
        compiler_params=pltpu.CompilerParams(
            collective_id=0, has_side_effects=True, vmem_limit_bytes=40 * 1024 * 1024
        ),
        name="update",
    )(
        member_rows, perturbations, diffusivity, sea_mask,
        as_rows(obs_owner), as_rows(obs_cell), as_rows(obs_depart), as_rows(obs_weight),
    )
    return increment, residual.reshape(count)


def solution(mesh):
    sizes = tuple(mesh.shape[name] for name in ("lat", "lon", "mem"))
    return jax.shard_map(
        functools.partial(per_device, sizes),
        mesh=mesh,
        in_specs=(
            P("mem", "lat", "lon"),
            P("lat", "lon"),
            P("lat", "lon"),
            P(("lat", "lon", "mem"), None),
            P(("lat", "lon", "mem")),
            P(("lat", "lon", "mem")),
            P(("lat", "lon", "mem")),
        ),
        out_specs=(P("lat", "lon"), P(("lat", "lon", "mem"))),
        check_vma=False,
    )
```

```python
import functools

import jax
import jax.numpy as jnp
from jax import lax
from jax.experimental import pallas as pl
from jax.experimental.pallas import tpu as pltpu
from jax.sharding import PartitionSpec as P

STEPS = 4
LANES = 128
RIM = 8
F32 = jnp.float32
BF16 = jnp.bfloat16
MESH = pl.DeviceIdType.MESH
DIRECTIONS = [(0, 1), (0, -1), (1, 0), (-1, 0), (1, 1), (1, -1), (-1, 1), (-1, -1)]
EVERY = range(8)
SIDES = (0, 1, 4, 5, 6, 7)
AHEAD = (2, 3)
WIDE = {0: (pl.ds(0, 256), pl.ds(0, 256)), 1: (pl.ds(128, 128), pl.ds(384, 128)), -1: (pl.ds(0, 128), pl.ds(256, 128))}
NARROW = {1: (pl.ds(0, 128), pl.ds(256, 128)), -1: (pl.ds(0, 128), pl.ds(128, 128))}


def halves(value):
    high = value.astype(BF16).astype(F32)
    return high, value - high


def dot_nt(left, right):
    return lax.dot_general(left, right, (((1,), (1,)), ((), ())), preferred_element_type=F32)


def dot_nn(left, right):
    return lax.dot_general(left, right, (((1,), (0,)), ((), ())), preferred_element_type=F32)


def rows_iota(count):
    return lax.broadcasted_iota(jnp.int32, (count, LANES), 0)


def one_hot(index_row, count):
    return jnp.where(rows_iota(count) == index_row, 1.0, 0.0).astype(BF16)


def kernel(
    sizes,
    member_ref, plain_ref, rate_ref, sea_ref, owner_ref, cell_ref, depart_ref, weight_ref,
    increment_ref, residual_ref,
    member_all, edge_ext, coef_ext, source1, source2, spread, north_all, east_all, west_all,
    outgoing, arrived, partial1, partial, gathered1, gathered2, gathered3, kept, answers, returned,
    rank_ref, total_ref, wide_ref, lane_hot, column_hot,
    send_x, recv_x, send_e, recv_e, send_c, recv_c, send_v1, recv_v1, send_v2, recv_v2, sums_sem, a2a_sem,
):
    lat_size, lon_size, mem_size, places, q, block_rows, divisor = sizes
    tile_rows, tile_cols = rate_ref.shape
    chunks = owner_ref.shape[0]
    lat = lax.axis_index("lat")
    lon = lax.axis_index("lon")
    mem = lax.axis_index("mem")
    place = lat * lon_size + lon
    quarter = tile_rows // mem_size
    shift_q = q.bit_length() - 1
    shift_b = block_rows.bit_length() - 1
    end = RIM + tile_rows
    ext_rows = tile_rows + 2 * RIM

    def place_at(step):
        other = lax.rem(place + step, places)
        return other, (other // lon_size, lax.rem(other, lon_size), mem)

    barrier = pltpu.get_barrier_semaphore()

    def greet(step, carry):
        pl.semaphore_signal(barrier, inc=1, device_id=place_at(step)[1], device_id_type=MESH)
        return carry

    lax.fori_loop(1, places, greet, 0)
    for step in range(1, mem_size):
        pl.semaphore_signal(
            barrier, inc=1, device_id=(lat, lon, lax.rem(mem + step, mem_size)), device_id_type=MESH
        )

    zero_rows = jnp.zeros((RIM, 512), F32)
    for ext in (source1, source2, coef_ext.at[0], coef_ext.at[1]):
        @pl.when(lat == 0)
        def _(ext=ext):
            ext[0:RIM, :] = zero_rows

        @pl.when(lat == lat_size - 1)
        def _(ext=ext):
            ext[end:ext_rows, :] = zero_rows

    @pl.when(lat == 0)
    def _():
        member_all[0:RIM] = jnp.zeros((RIM, 8, 384), F32)
        edge_ext[0:RIM] = jnp.zeros((RIM, 3 * LANES), F32)

    @pl.when(lat == lat_size - 1)
    def _():
        member_all[end:ext_rows] = jnp.zeros((RIM, 8, 384), F32)
        edge_ext[end:ext_rows] = jnp.zeros((RIM, 3 * LANES), F32)

    member_all[0:4, :, 0:tile_cols] = jnp.zeros((4, 8, tile_cols), F32)
    member_all[end + 4 : ext_rows, :, 0:tile_cols] = jnp.zeros((4, 8, tile_cols), F32)
    member_all[RIM:end, :, 0:tile_cols] = member_ref[...]
    lane = lax.broadcasted_iota(jnp.int32, (1, LANES), 1)
    edges = jnp.zeros((tile_rows, LANES), F32)
    for m in range(8):
        middle = 8 * (8 - m)
        first_cols = plain_ref[m, :, 0:LANES].astype(F32)
        last_cols = plain_ref[m, :, tile_cols - LANES : tile_cols].astype(F32)
        turned = pltpu.roll(jnp.where(lane < 64, first_cols, last_cols), middle, 1)
        edges = jnp.where((lane >= middle - 4) & (lane < middle + 4), turned, edges)
    edge_ext[RIM:end, 0:LANES] = edges
    coef_ext[0, RIM:end, 0:tile_cols] = rate_ref[...]
    coef_ext[1, RIM:end, 0:tile_cols] = sea_ref[...].astype(F32)

    pl.semaphore_wait(barrier, places - 1 + mem_size - 1)

    def halo_copies(at, send_sem, recv_sem, directions, depth=RIM, cols=None):
        made = []
        for k in directions:
            dy, dx = DIRECTIONS[k]
            source_rows = {0: pl.ds(RIM, tile_rows), 1: pl.ds(end - depth, depth), -1: pl.ds(RIM, depth)}[dy]
            target_rows = {0: pl.ds(RIM, tile_rows), 1: pl.ds(RIM - depth, depth), -1: pl.ds(end, depth)}[dy]
            source_cols, target_cols = (cols or WIDE)[dx]
            copy = pltpu.make_async_remote_copy(
                src_ref=at(source_rows, source_cols),
                dst_ref=at(target_rows, target_cols),
                send_sem=send_sem.at[k],
                recv_sem=recv_sem.at[k],
                device_id=(lat + dy, lax.rem(lon + dx + lon_size, lon_size), mem),
                device_id_type=MESH,
            )
            sends = {0: None, 1: lat < lat_size - 1, -1: lat > 0}[dy]
            gets = {0: None, 1: lat > 0, -1: lat < lat_size - 1}[dy]
            made.append((copy, sends, gets))
        return made

    def when(condition, action):
        if condition is None:
            action()
        else:
            pl.when(condition)(action)

    def halo_start(copies):
        for copy, sends, gets in copies:
            when(sends, lambda copy=copy: copy.start())

    sent = []

    def halo_wait(copies):
        for copy, sends, gets in copies:
            when(gets, lambda copy=copy: copy.wait_recv())
            sent.append(lambda copy=copy, sends=sends: when(sends, lambda: copy.wait_send()))

    coef_copies = halo_copies(lambda r, c: coef_ext.at[:, r, c], send_c, recv_c, EVERY)
    edge_copies = halo_copies(lambda r, c: edge_ext.at[r, c], send_e, recv_e, SIDES, cols=NARROW)
    member_copies = halo_copies(lambda r, c: member_all.at[r, :, c], send_x, recv_x, AHEAD, depth=4)
    source_copies = [
        halo_copies(lambda r, c: source1.at[r, c], send_v1, recv_v1, EVERY),
        halo_copies(lambda r, c: source2.at[r, c], send_v2, recv_v2, EVERY),
    ]

    owner = owner_ref[...]
    upper = jnp.where(
        lax.broadcasted_iota(jnp.int32, (LANES, LANES), 0)
        < lax.broadcasted_iota(jnp.int32, (LANES, LANES), 1), 1.0, 0.0,
    ).astype(BF16)
    table = jnp.concatenate([upper, jnp.ones((LANES, LANES), BF16)], axis=1)
    before = jnp.zeros((places, LANES), F32)
    match = jnp.concatenate(
        [jnp.where(rows_iota(places) == owner[r : r + 1], 1.0, 0.0) for r in range(chunks)], axis=0
    )
    counts = dot_nn(match.astype(BF16), table)
    for r in range(chunks):
        part = slice(r * places, (r + 1) * places)
        found = jnp.sum(match[part] * (counts[part, :LANES] + before), axis=0, keepdims=True)
        rank_ref[r : r + 1, :] = found.astype(jnp.int32)
        before = before + counts[part, LANES:]
    rank = rank_ref[...]
    slot_row = owner * block_rows + lax.shift_right_logical(rank, 7)
    slot_lane = lax.bitwise_and(rank, 127)

    depart = depart_ref[...]
    weight = weight_ref[...]
    cell = cell_ref[...]
    product1, product2 = halves(weight * depart)
    weight1, weight2 = halves(weight)
    cell2 = lax.bitwise_and(cell, 127)
    cell1 = (cell - cell2).astype(F32)
    cell2 = cell2.astype(F32)
    pack_rows = places * block_rows
    row = rows_iota(pack_rows)
    inner = lax.bitwise_and(row, block_rows - 1)
    field = lax.shift_right_logical(inner, shift_q)
    base_row = row - lax.shift_left(field, shift_q)
    packed = jnp.zeros((2 * pack_rows, LANES), F32)
    for r in range(0, chunks, 4):
        lefts = []
        for c in range(r, r + 4):
            s = slice(c, c + 1)
            hit = base_row == slot_row[s]
            parts = [
                jnp.where(field == 0, of_product[s], jnp.where(field == 1, of_weight[s], of_cell[s]))
                for of_product, of_weight, of_cell in ((product1, weight1, cell1), (product2, weight2, cell2))
            ]
            lefts.append(jnp.concatenate([jnp.where(hit, p, 0.0) for p in parts], axis=0).astype(BF16))
            lane_hot[:, c * LANES : (c + 1) * LANES] = one_hot(slot_lane[s], LANES)
        right = lane_hot[:, r * LANES : (r + 4) * LANES]
        packed = packed + dot_nt(jnp.concatenate(lefts, axis=1), right)
    packed = packed[:pack_rows] + packed[pack_rows:]
    outgoing[...] = packed.reshape(places, block_rows, LANES)

    def exchange(from_ref, to_ref, sems):
        def send(step, carry):
            other, device = place_at(step)
            pltpu.make_async_remote_copy(
                src_ref=from_ref.at[other], dst_ref=to_ref.at[place],
                send_sem=sems.at[0], recv_sem=sems.at[1],
                device_id=device, device_id_type=MESH,
            ).start()
            return carry

        lax.fori_loop(1, places, send, 0)

    def exchange_wait(from_ref, to_ref, sems):
        whole = pltpu.make_async_remote_copy(
            src_ref=from_ref.at[pl.ds(0, places - 1)], dst_ref=to_ref.at[pl.ds(0, places - 1)],
            send_sem=sems.at[0], recv_sem=sems.at[1],
            device_id=place_at(1)[1], device_id_type=MESH,
        )
        whole.wait_recv()
        sent.append(whole.wait_send)

    exchange(outgoing, arrived, a2a_sem.at[0])
    halo_start(coef_copies)
    halo_start(edge_copies)
    halo_start(member_copies)
    arrived[place] = outgoing[place]
    exchange_wait(outgoing, arrived, a2a_sem.at[0])

    def slot_cells(block):
        whole = block[2 * q : 3 * q].astype(jnp.int32)
        return lax.shift_right_logical(whole, 8), lax.bitwise_and(whole, 255)

    total_ref[...] = jnp.zeros_like(total_ref)
    group = 4
    span = q * LANES

    def add_blocks(step, carry):
        lefts, rights = [], []
        for u in range(group):
            block = arrived[step * group + u]
            high, low = slot_cells(block)
            for k in range(q):
                hit = rows_iota(tile_rows) == high[k : k + 1]
                parts = halves(block[k : k + 1]) + halves(block[q + k : q + k + 1])
                lefts.append(jnp.concatenate([jnp.where(hit, p, 0.0) for p in parts], axis=0).astype(BF16))
                rights.append(one_hot(low[k : k + 1], tile_cols))
        right = jnp.concatenate(rights, axis=1)
        column_hot[step] = right
        total_ref[...] += dot_nt(jnp.concatenate(lefts, axis=1), right)
        return carry

    lax.fori_loop(0, places // group, add_blocks, 0)
    for f in range(2):
        start = 2 * f * tile_rows
        partial1[f] = total_ref[start : start + tile_rows, :] + total_ref[start + tile_rows : start + 2 * tile_rows, :]

    my_rows = pl.multiple_of(mem * quarter, quarter)

    def sum_copy(part_at, got, number, other):
        sems = sums_sem.at[2 * number]
        return pltpu.make_async_remote_copy(
            src_ref=part_at(pl.ds(pl.multiple_of(other * quarter, quarter), quarter)),
            dst_ref=got.at[mem],
            send_sem=sems.at[0], recv_sem=sems.at[1],
            device_id=(lat, lon, other), device_id_type=MESH,
        )

    def sum_part(part_at, got, number, other):
        @pl.when(mem != other)
        def _():
            sum_copy(part_at, got, number, other).start()

    def member_sum(part_at, got, number):
        sems = sums_sem.at[2 * number]
        got[mem] = part_at(pl.ds(my_rows, quarter))[...]
        whole = pltpu.make_async_remote_copy(
            src_ref=got.at[pl.ds(0, mem_size - 1)], dst_ref=got.at[pl.ds(0, mem_size - 1)],
            send_sem=sems.at[0], recv_sem=sems.at[1],
            device_id=(lat, lon, lax.rem(mem + 1, mem_size)), device_id_type=MESH,
        )
        whole.wait_recv()
        sent.append(whole.wait_send)
        total = got[0]
        for other in range(1, mem_size):
            total = total + got[other]
        return total

    def member_share(ref, first, number):
        sems = sums_sem.at[2 * number + 1]
        mine = ref.at[pl.ds(first + my_rows, quarter), pl.ds(0, tile_cols)]
        for step in range(1, mem_size):
            pltpu.make_async_remote_copy(
                src_ref=mine, dst_ref=mine,
                send_sem=sems.at[0], recv_sem=sems.at[1],
                device_id=(lat, lon, lax.rem(mem + step, mem_size)), device_id_type=MESH,
            ).start()
        rest = ref.at[pl.ds(first, (mem_size - 1) * quarter), pl.ds(0, tile_cols)]
        whole = pltpu.make_async_remote_copy(
            src_ref=rest, dst_ref=rest, send_sem=sems.at[0], recv_sem=sems.at[1],
            device_id=(lat, lon, lax.rem(mem + 1, mem_size)), device_id_type=MESH,
        )
        whole.wait_recv()
        sent.append(whole.wait_send)

    first_part = lambda rows: partial1.at[:, rows]
    for step in range(1, mem_size):
        sum_copy(first_part, gathered1, 0, lax.rem(mem + step, mem_size)).start()
    summed = member_sum(first_part, gathered1, 0)
    kept[...] = summed
    source1[pl.ds(RIM + my_rows, quarter), 0:tile_cols] = summed[0]
    member_share(source1, RIM, 0)
    halo_start(source_copies[0])


    def joined(value):
        side = jnp.where(lane < 64, value[..., 256:384], value[..., 384:512])
        return jnp.concatenate([value[..., 0:256], side], axis=-1)

    halo_wait(coef_copies)
    halo_wait(edge_copies)
    halo_wait(member_copies)
    rate = joined(coef_ext[0])
    sea = joined(coef_ext[1])
    below = lambda a: jnp.concatenate([a[1:], a[:1]], axis=0)
    width = 384
    wide_ref[0] = 0.5 * (rate + below(rate)) * sea * below(sea)
    wide_ref[1] = 0.5 * (rate + pltpu.roll(rate, width - 1, 1)) * sea * pltpu.roll(sea, width - 1, 1)

    wide_ref[2] = pltpu.roll(wide_ref[1], 1, 1)

    def widen(step, carry):
        base = pl.multiple_of(step * 8, 8)
        for u in range(8):
            i = base + u
            north_all[i] = jnp.broadcast_to(wide_ref[0, pl.ds(i, 1), :], (8, width))
            east_all[i] = jnp.broadcast_to(wide_ref[1, pl.ds(i, 1), :], (8, width))
            west_all[i] = jnp.broadcast_to(wide_ref[2, pl.ds(i, 1), :], (8, width))
            line = edge_ext[pl.ds(i, 1), :]
            both = jnp.where(lax.bitwise_and(lane, 7) < 4, line[:, 128:256], line[:, 256:384])
            member_all[i, :, 256:384] = pltpu.roll(
                jnp.broadcast_to(both, (8, LANES)), 64, 1, stride=8, stride_axis=0
            )
        return carry

    lax.fori_loop(0, ext_rows // 8, widen, 0)

    def covariance(source, finished):
        wide_ref[0] = joined(source[...])

        def step_rows(read, base, carry, count):
            here, flux = carry
            values = [here] + [read(base + u + 1) for u in range(count)]
            results = []
            for u in range(count):
                here, after = values[u], values[u + 1]
                flux_after = north_all[base + u] * (after - here)
                flux_east = east_all[base + u] * (pltpu.roll(here, width - 1, 1) - here)
                flux_west = west_all[base + u] * (pltpu.roll(here, 1, 1) - here)
                results.append(here + (flux_after - flux) + (flux_east + flux_west))
                flux = flux_after
            return results, (values[-1], flux)

        def first_of(read, row):
            here = read(row)
            return here, north_all[row - 1] * (here - read(row - 1))

        def sweep(read):
            def rows(step, carry):
                base = 4 + step * 24
                results, carry = step_rows(read, base, carry, 24)
                for u in range(24):
                    spread[base + u] = results[u]
                return carry

            lax.fori_loop(0, (tile_rows + 8) // 24, rows, first_of(read, 4))

        def begin(i):
            return member_all[i] * wide_ref[0, pl.ds(i, 1), :]

        def again(i):
            return spread[i]

        spread[3] = begin(3)
        spread[tile_rows + 12] = begin(tile_rows + 12)
        sweep(begin)
        for turn in range(STEPS - 2):
            sweep(again)

        carry = first_of(again, RIM)
        for part in range(mem_size):
            base = RIM + part * quarter
            results, carry = step_rows(again, base, carry, quarter)
            found = [
                jnp.sum(results[u][:, 0:256] * member_all[base + u, :, 0:256], axis=0, keepdims=True)
                for u in range(quarter)
            ]
            partial[part * quarter : (part + 1) * quarter, :] = jnp.concatenate(found, axis=0)
            finished(part)

    my_sea = lambda: coef_ext[1, pl.ds(RIM + my_rows, quarter), 0:tile_cols]
    halo_wait(source_copies[0])
    later_part = lambda rows: partial.at[rows]
    covariance(source1, lambda part: sum_part(later_part, gathered2, 1, part))
    first_total = member_sum(later_part, gathered2, 1)
    sum_sent = sent.pop()
    first_pass = my_sea() * first_total / divisor
    source2[pl.ds(RIM + my_rows, quarter), 0:tile_cols] = kept[0] - kept[1] * first_pass
    member_share(source2, RIM, 1)
    halo_start(source_copies[1])
    halo_wait(source_copies[1])
    sum_sent()
    covariance(source2, lambda part: sum_part(later_part, gathered3, 2, part))
    wide = my_sea() * member_sum(later_part, gathered3, 2) / divisor
    increment_ref[pl.ds(my_rows, quarter), :] = wide
    member_share(increment_ref, 0, 2)

    first, second = halves(increment_ref[...])
    lookup = jnp.concatenate([first, second], axis=0).astype(BF16)

    def look(step, carry):
        got = dot_nn(lookup, column_hot[step])
        value = got[:tile_rows] + got[tile_rows:]
        for u in range(group):
            origin = step * group + u
            high, low = slot_cells(arrived[origin])
            found = []
            for k in range(q):
                hit = rows_iota(tile_rows) == high[k : k + 1]
                start = u * span + k * LANES
                part = value[:, start : start + LANES]
                found.append(jnp.sum(jnp.where(hit, part, 0.0), axis=0, keepdims=True))
            found.append(jnp.zeros((8 - q, LANES), F32))
            answers[origin] = jnp.concatenate(found, axis=0)
        return carry

    lax.fori_loop(0, places // group, look, 0)
    exchange(answers, returned, a2a_sem.at[1])
    returned[place] = answers[place]
    exchange_wait(answers, returned, a2a_sem.at[1])
    first, second = halves(returned[...].reshape(places * 8, LANES))
    lookup = jnp.concatenate([first, second], axis=0).astype(BF16)
    answer_row = owner * 8 + lax.shift_right_logical(rank_ref[...], 7)
    got = dot_nn(lookup, lane_hot[...])
    values = got[: places * 8] + got[places * 8 :]
    for r in range(chunks):
        value = values[:, r * LANES : (r + 1) * LANES]
        hit = rows_iota(places * 8) == answer_row[r : r + 1]
        found = jnp.sum(jnp.where(hit, value, 0.0), axis=0, keepdims=True)
        residual_ref[r : r + 1, :] = depart_ref[r : r + 1, :] - found
    for wait in sent:
        wait()


def per_device(sizes, perturbations, diffusivity, sea_mask, obs_owner, obs_cell, obs_depart, obs_weight):
    lat_size, lon_size, mem_size = sizes
    members, tile_rows, tile_cols = perturbations.shape
    count = obs_cell.shape[0]
    places = lat_size * lon_size
    capacity = max(2, 2 * count // places)
    q = max(1, capacity // LANES)
    block_rows = 8
    while block_rows < 3 * q:
        block_rows *= 2
    rows = count // LANES
    ext = tile_rows + 2 * RIM
    quarter = tile_rows // mem_size
    divisor = members * mem_size - 1
    vmem = pltpu.VMEM
    dma = pltpu.SemaphoreType.DMA
    as_rows = lambda a: a.reshape(rows, LANES)
    member_rows = jnp.transpose(perturbations, (1, 0, 2)).astype(F32)
    increment, residual = pl.pallas_call(
        functools.partial(kernel, (lat_size, lon_size, mem_size, places, q, block_rows, divisor)),
        out_shape=(
            jax.ShapeDtypeStruct((tile_rows, tile_cols), F32),
            jax.ShapeDtypeStruct((rows, LANES), F32),
        ),
        in_specs=[pl.BlockSpec(memory_space=vmem)] * 8,
        out_specs=(pl.BlockSpec(memory_space=vmem),) * 2,
        scratch_shapes=[
            vmem((ext, 8, 384), F32),
            vmem((ext, 3 * LANES), F32),
            vmem((2, ext, 512), F32),
            vmem((ext, 512), F32),
            vmem((ext, 512), F32),
            vmem((ext, 8, 384), F32),
            vmem((ext, 8, 384), F32),
            vmem((ext, 8, 384), F32),
            vmem((ext, 8, 384), F32),
            vmem((places, block_rows, LANES), F32),
            vmem((places, block_rows, LANES), F32),
            vmem((2, tile_rows, tile_cols), F32),
            vmem((tile_rows, tile_cols), F32),
            vmem((mem_size, 2, quarter, tile_cols), F32),
            vmem((mem_size, quarter, tile_cols), F32),
            vmem((mem_size, quarter, tile_cols), F32),
            vmem((2, quarter, tile_cols), F32),
            vmem((places, 8, LANES), F32),
            vmem((places, 8, LANES), F32),
            vmem((rows, LANES), jnp.int32),
            vmem((4 * tile_rows, tile_cols), F32),
            vmem((3, ext, 384), F32),
            vmem((LANES, count), BF16),
            vmem((places // 4, tile_cols, 4 * q * LANES), BF16),
        ] + [dma((8,))] * 10 + [dma((6, 2)), dma((2, 2))],
        compiler_params=pltpu.CompilerParams(
            collective_id=0, has_side_effects=True, vmem_limit_bytes=40 * 1024 * 1024
        ),
        name="update",
    )(
        member_rows, perturbations, diffusivity, sea_mask,
        as_rows(obs_owner), as_rows(obs_cell), as_rows(obs_depart), as_rows(obs_weight),
    )
    return increment, residual.reshape(count)


def solution(mesh):
    sizes = tuple(mesh.shape[name] for name in ("lat", "lon", "mem"))
    return jax.shard_map(
        functools.partial(per_device, sizes),
        mesh=mesh,
        in_specs=(
            P("mem", "lat", "lon"),
            P("lat", "lon"),
            P("lat", "lon"),
            P(("lat", "lon", "mem"), None),
            P(("lat", "lon", "mem")),
            P(("lat", "lon", "mem")),
            P(("lat", "lon", "mem")),
        ),
        out_specs=(P("lat", "lon"), P(("lat", "lon", "mem"))),
        check_vma=False,
    )
```

```python
import functools

import jax
import jax.numpy as jnp
from jax import lax
from jax.experimental import pallas as pl
from jax.experimental.pallas import tpu as pltpu
from jax.sharding import PartitionSpec as P

STEPS = 4
LANES = 128
RIM = 8
F32 = jnp.float32
BF16 = jnp.bfloat16
MESH = pl.DeviceIdType.MESH
DIRECTIONS = [(0, 1), (0, -1), (1, 0), (-1, 0), (1, 1), (1, -1), (-1, 1), (-1, -1)]
EVERY = range(8)
SIDES = (0, 1, 4, 5, 6, 7)
AHEAD = (2, 3)
WIDE = {0: (pl.ds(0, 256), pl.ds(0, 256)), 1: (pl.ds(128, 128), pl.ds(384, 128)), -1: (pl.ds(0, 128), pl.ds(256, 128))}
NARROW = {1: (pl.ds(0, 128), pl.ds(256, 128)), -1: (pl.ds(0, 128), pl.ds(128, 128))}


def halves(value):
    high = value.astype(BF16).astype(F32)
    return high, value - high


def dot_nt(left, right):
    return lax.dot_general(left, right, (((1,), (1,)), ((), ())), preferred_element_type=F32)


def dot_nn(left, right):
    return lax.dot_general(left, right, (((1,), (0,)), ((), ())), preferred_element_type=F32)


def rows_iota(count):
    return lax.broadcasted_iota(jnp.int32, (count, LANES), 0)


def one_hot(index_row, count):
    return jnp.where(rows_iota(count) == index_row, 1.0, 0.0).astype(BF16)


def kernel(
    sizes,
    member_ref, plain_ref, rate_ref, sea_ref, owner_ref, cell_ref, depart_ref, weight_ref,
    increment_ref, residual_ref,
    member_all, edge_ext, coef_ext, source1, source2, spread, north_all, east_all, west_all,
    outgoing, arrived, partial1, partial, gathered1, gathered2, gathered3, kept, answers, returned,
    rank_ref, total_ref, wide_ref, lane_hot, column_hot,
    send_x, recv_x, send_e, recv_e, send_c, recv_c, send_v1, recv_v1, send_v2, recv_v2, sums_sem, a2a_sem,
):
    lat_size, lon_size, mem_size, places, q, block_rows, divisor = sizes
    tile_rows, tile_cols = rate_ref.shape
    chunks = owner_ref.shape[0]
    lat = lax.axis_index("lat")
    lon = lax.axis_index("lon")
    mem = lax.axis_index("mem")
    place = lat * lon_size + lon
    quarter = tile_rows // mem_size
    shift_q = q.bit_length() - 1
    shift_b = block_rows.bit_length() - 1
    end = RIM + tile_rows
    ext_rows = tile_rows + 2 * RIM

    def place_at(step):
        other = lax.rem(place + step, places)
        return other, (other // lon_size, lax.rem(other, lon_size), mem)

    def when(condition, action):
        if condition is None:
            action()
        else:
            pl.when(condition)(action)

    def neighbour(dy, dx, member):
        return lat + dy, lax.rem(lon + dx + lon_size, lon_size), member

    barrier = pltpu.get_barrier_semaphore()

    def greet(step, carry):
        pl.semaphore_signal(barrier, inc=1, device_id=place_at(step)[1], device_id_type=MESH)
        return carry

    lax.fori_loop(1, places, greet, 0)
    for step in range(1, mem_size):
        pl.semaphore_signal(
            barrier, inc=1, device_id=(lat, lon, lax.rem(mem + step, mem_size)), device_id_type=MESH
        )

    exists = {0: None, 1: lat < lat_size - 1, -1: lat > 0}
    for dy, dx in DIRECTIONS:
        for step in range(1, mem_size):
            when(exists[dy], lambda dy=dy, dx=dx, step=step: pl.semaphore_signal(
                barrier, inc=1, device_id=neighbour(dy, dx, lax.rem(mem + step, mem_size)), device_id_type=MESH
            ))

    zero_rows = jnp.zeros((RIM, 512), F32)
    for ext in (source1, source2, coef_ext.at[0], coef_ext.at[1]):
        @pl.when(lat == 0)
        def _(ext=ext):
            ext[0:RIM, :] = zero_rows

        @pl.when(lat == lat_size - 1)
        def _(ext=ext):
            ext[end:ext_rows, :] = zero_rows

    @pl.when(lat == 0)
    def _():
        member_all[0:RIM] = jnp.zeros((RIM, 8, 384), F32)
        edge_ext[0:RIM] = jnp.zeros((RIM, 3 * LANES), F32)

    @pl.when(lat == lat_size - 1)
    def _():
        member_all[end:ext_rows] = jnp.zeros((RIM, 8, 384), F32)
        edge_ext[end:ext_rows] = jnp.zeros((RIM, 3 * LANES), F32)

    member_all[0:4, :, 0:tile_cols] = jnp.zeros((4, 8, tile_cols), F32)
    member_all[end + 4 : ext_rows, :, 0:tile_cols] = jnp.zeros((4, 8, tile_cols), F32)
    member_all[RIM:end, :, 0:tile_cols] = member_ref[...]
    lane = lax.broadcasted_iota(jnp.int32, (1, LANES), 1)
    edges = jnp.zeros((tile_rows, LANES), F32)
    for m in range(8):
        middle = 8 * (8 - m)
        first_cols = plain_ref[m, :, 0:LANES].astype(F32)
        last_cols = plain_ref[m, :, tile_cols - LANES : tile_cols].astype(F32)
        turned = pltpu.roll(jnp.where(lane < 64, first_cols, last_cols), middle, 1)
        edges = jnp.where((lane >= middle - 4) & (lane < middle + 4), turned, edges)
    edge_ext[RIM:end, 0:LANES] = edges
    coef_ext[0, RIM:end, 0:tile_cols] = rate_ref[...]
    coef_ext[1, RIM:end, 0:tile_cols] = sea_ref[...].astype(F32)

    def halo_copies(at, send_sem, recv_sem, directions, depth=RIM, cols=None):
        made = []
        for k in directions:
            dy, dx = DIRECTIONS[k]
            source_rows = {0: pl.ds(RIM, tile_rows), 1: pl.ds(end - depth, depth), -1: pl.ds(RIM, depth)}[dy]
            target_rows = {0: pl.ds(RIM, tile_rows), 1: pl.ds(RIM - depth, depth), -1: pl.ds(end, depth)}[dy]
            source_cols, target_cols = (cols or WIDE)[dx]
            copy = pltpu.make_async_remote_copy(
                src_ref=at(source_rows, source_cols),
                dst_ref=at(target_rows, target_cols),
                send_sem=send_sem.at[k],
                recv_sem=recv_sem.at[k],
                device_id=neighbour(dy, dx, mem),
                device_id_type=MESH,
            )
            sends = {0: None, 1: lat < lat_size - 1, -1: lat > 0}[dy]
            gets = {0: None, 1: lat > 0, -1: lat < lat_size - 1}[dy]
            made.append((copy, sends, gets))
        return made

    def halo_start(copies):
        for copy, sends, gets in copies:
            when(sends, lambda copy=copy: copy.start())

    sent = []

    def halo_wait(copies):
        for copy, sends, gets in copies:
            when(gets, lambda copy=copy: copy.wait_recv())
            sent.append(lambda copy=copy, sends=sends: when(sends, lambda: copy.wait_send()))

    coef_copies = halo_copies(lambda r, c: coef_ext.at[:, r, c], send_c, recv_c, EVERY)
    edge_copies = halo_copies(lambda r, c: edge_ext.at[r, c], send_e, recv_e, SIDES, cols=NARROW)
    member_copies = halo_copies(lambda r, c: member_all.at[r, :, c], send_x, recv_x, AHEAD, depth=4)
    source_copies = [
        halo_copies(lambda r, c: source1.at[r, c], send_v1, recv_v1, EVERY),
        halo_copies(lambda r, c: source2.at[r, c], send_v2, recv_v2, EVERY),
    ]

    owner = owner_ref[...]
    upper = jnp.where(
        lax.broadcasted_iota(jnp.int32, (LANES, LANES), 0)
        < lax.broadcasted_iota(jnp.int32, (LANES, LANES), 1), 1.0, 0.0,
    ).astype(BF16)
    table = jnp.concatenate([upper, jnp.ones((LANES, LANES), BF16)], axis=1)
    before = jnp.zeros((places, LANES), F32)
    match = jnp.concatenate(
        [jnp.where(rows_iota(places) == owner[r : r + 1], 1.0, 0.0) for r in range(chunks)], axis=0
    )
    counts = dot_nn(match.astype(BF16), table)
    for r in range(chunks):
        part = slice(r * places, (r + 1) * places)
        found = jnp.sum(match[part] * (counts[part, :LANES] + before), axis=0, keepdims=True)
        rank_ref[r : r + 1, :] = found.astype(jnp.int32)
        before = before + counts[part, LANES:]
    rank = rank_ref[...]
    slot_row = owner * block_rows + lax.shift_right_logical(rank, 7)
    slot_lane = lax.bitwise_and(rank, 127)

    depart = depart_ref[...]
    weight = weight_ref[...]
    cell = cell_ref[...]
    product1, product2 = halves(weight * depart)
    weight1, weight2 = halves(weight)
    cell2 = lax.bitwise_and(cell, 127)
    cell1 = (cell - cell2).astype(F32)
    cell2 = cell2.astype(F32)
    pack_rows = places * block_rows
    row = rows_iota(pack_rows)
    inner = lax.bitwise_and(row, block_rows - 1)
    field = lax.shift_right_logical(inner, shift_q)
    base_row = row - lax.shift_left(field, shift_q)
    packed = jnp.zeros((2 * pack_rows, LANES), F32)
    for r in range(0, chunks, 4):
        lefts = []
        for c in range(r, r + 4):
            s = slice(c, c + 1)
            hit = base_row == slot_row[s]
            parts = [
                jnp.where(field == 0, of_product[s], jnp.where(field == 1, of_weight[s], of_cell[s]))
                for of_product, of_weight, of_cell in ((product1, weight1, cell1), (product2, weight2, cell2))
            ]
            lefts.append(jnp.concatenate([jnp.where(hit, p, 0.0) for p in parts], axis=0).astype(BF16))
            lane_hot[:, c * LANES : (c + 1) * LANES] = one_hot(slot_lane[s], LANES)
        right = lane_hot[:, r * LANES : (r + 4) * LANES]
        packed = packed + dot_nt(jnp.concatenate(lefts, axis=1), right)
    packed = packed[:pack_rows] + packed[pack_rows:]
    outgoing[...] = packed.reshape(places, block_rows, LANES)

    def exchange(from_ref, to_ref, sems):
        def send(step, carry):
            other, device = place_at(step)
            pltpu.make_async_remote_copy(
                src_ref=from_ref.at[other], dst_ref=to_ref.at[place],
                send_sem=sems.at[0], recv_sem=sems.at[1],
                device_id=device, device_id_type=MESH,
            ).start()
            return carry

        lax.fori_loop(1, places, send, 0)

    def exchange_wait(from_ref, to_ref, sems):
        whole = pltpu.make_async_remote_copy(
            src_ref=from_ref.at[pl.ds(0, places - 1)], dst_ref=to_ref.at[pl.ds(0, places - 1)],
            send_sem=sems.at[0], recv_sem=sems.at[1],
            device_id=place_at(1)[1], device_id_type=MESH,
        )
        whole.wait_recv()
        sent.append(whole.wait_send)

    tiles = 2 + 3 * (jnp.where(lat > 0, 1, 0) + jnp.where(lat < lat_size - 1, 1, 0))
    pl.semaphore_wait(barrier, places - 1 + (mem_size - 1) * (tiles + 1))
    exchange(outgoing, arrived, a2a_sem.at[0])
    halo_start(coef_copies)
    halo_start(edge_copies)
    halo_start(member_copies)
    arrived[place] = outgoing[place]
    exchange_wait(outgoing, arrived, a2a_sem.at[0])

    def slot_cells(block):
        whole = block[2 * q : 3 * q].astype(jnp.int32)
        return lax.shift_right_logical(whole, 8), lax.bitwise_and(whole, 255)

    total_ref[...] = jnp.zeros_like(total_ref)
    group = 4
    span = q * LANES

    def add_blocks(step, carry):
        lefts, rights = [], []
        for u in range(group):
            block = arrived[step * group + u]
            high, low = slot_cells(block)
            for k in range(q):
                hit = rows_iota(tile_rows) == high[k : k + 1]
                parts = halves(block[k : k + 1]) + halves(block[q + k : q + k + 1])
                lefts.append(jnp.concatenate([jnp.where(hit, p, 0.0) for p in parts], axis=0).astype(BF16))
                rights.append(one_hot(low[k : k + 1], tile_cols))
        right = jnp.concatenate(rights, axis=1)
        column_hot[step] = right
        total_ref[...] += dot_nt(jnp.concatenate(lefts, axis=1), right)
        return carry

    lax.fori_loop(0, places // group, add_blocks, 0)
    for f in range(2):
        start = 2 * f * tile_rows
        partial1[f] = total_ref[start : start + tile_rows, :] + total_ref[start + tile_rows : start + 2 * tile_rows, :]

    my_rows = pl.multiple_of(mem * quarter, quarter)

    def sum_copy(part_at, got, number, other):
        sems = sums_sem.at[2 * number]
        return pltpu.make_async_remote_copy(
            src_ref=part_at(pl.ds(pl.multiple_of(other * quarter, quarter), quarter)),
            dst_ref=got.at[mem],
            send_sem=sems.at[0], recv_sem=sems.at[1],
            device_id=(lat, lon, other), device_id_type=MESH,
        )

    def sum_part(part_at, got, number, other):
        @pl.when(mem != other)
        def _():
            sum_copy(part_at, got, number, other).start()

    def member_sum(part_at, got, number):
        sems = sums_sem.at[2 * number]
        got[mem] = part_at(pl.ds(my_rows, quarter))[...]
        whole = pltpu.make_async_remote_copy(
            src_ref=got.at[pl.ds(0, mem_size - 1)], dst_ref=got.at[pl.ds(0, mem_size - 1)],
            send_sem=sems.at[0], recv_sem=sems.at[1],
            device_id=(lat, lon, lax.rem(mem + 1, mem_size)), device_id_type=MESH,
        )
        whole.wait_recv()
        sent.append(whole.wait_send)
        total = got[0]
        for other in range(1, mem_size):
            total = total + got[other]
        return total

    def edge_share(ref, send_sem, recv_sem):
        own = pl.ds(RIM + my_rows, quarter)
        for k, (dy, dx) in enumerate(DIRECTIONS):
            source_rows = {0: own, 1: pl.ds(end - RIM, RIM), -1: pl.ds(RIM, RIM)}[dy]
            target_rows = {0: own, 1: pl.ds(0, RIM), -1: pl.ds(end, RIM)}[dy]
            source_cols, target_cols = WIDE[dx]
            sends = {0: None, 1: (lat < lat_size - 1) & (mem == mem_size - 1), -1: (lat > 0) & (mem == 0)}[dy]
            for step in range(mem_size):
                copy = pltpu.make_async_remote_copy(
                    src_ref=ref.at[source_rows, source_cols], dst_ref=ref.at[target_rows, target_cols],
                    send_sem=send_sem.at[k * mem_size + step], recv_sem=recv_sem.at[k],
                    device_id=neighbour(dy, dx, lax.rem(mem + step, mem_size)), device_id_type=MESH,
                )
                when(sends, lambda copy=copy: copy.start())
                sent.append(lambda copy=copy, sends=sends: when(sends, lambda: copy.wait_send()))

    def edge_wait(copies):
        for copy, sends, gets in copies:
            when(gets, lambda copy=copy: copy.wait_recv())

    def member_share(ref, first, number, meanwhile=lambda: None):
        sems = sums_sem.at[2 * number + 1]
        mine = ref.at[pl.ds(first + my_rows, quarter), pl.ds(0, tile_cols)]
        for step in range(1, mem_size):
            pltpu.make_async_remote_copy(
                src_ref=mine, dst_ref=mine,
                send_sem=sems.at[0], recv_sem=sems.at[1],
                device_id=(lat, lon, lax.rem(mem + step, mem_size)), device_id_type=MESH,
            ).start()
        meanwhile()
        rest = ref.at[pl.ds(first, (mem_size - 1) * quarter), pl.ds(0, tile_cols)]
        whole = pltpu.make_async_remote_copy(
            src_ref=rest, dst_ref=rest, send_sem=sems.at[0], recv_sem=sems.at[1],
            device_id=(lat, lon, lax.rem(mem + 1, mem_size)), device_id_type=MESH,
        )
        whole.wait_recv()
        sent.append(whole.wait_send)

    first_part = lambda rows: partial1.at[:, rows]
    for step in range(1, mem_size):
        sum_copy(first_part, gathered1, 0, lax.rem(mem + step, mem_size)).start()
    summed = member_sum(first_part, gathered1, 0)
    kept[...] = summed
    source1[pl.ds(RIM + my_rows, quarter), 0:tile_cols] = summed[0]

    width = 384

    def joined(value):
        side = jnp.where(lane < 64, value[..., 256:384], value[..., 384:512])
        return jnp.concatenate([value[..., 0:256], side], axis=-1)

    def prepare():
        edge_share(source1, send_v1, recv_v1)
        halo_wait(coef_copies)
        halo_wait(edge_copies)
        halo_wait(member_copies)
        rate = joined(coef_ext[0])
        sea = joined(coef_ext[1])
        below = lambda a: jnp.concatenate([a[1:], a[:1]], axis=0)
        wide_ref[0] = 0.5 * (rate + below(rate)) * sea * below(sea)
        wide_ref[1] = 0.5 * (rate + pltpu.roll(rate, width - 1, 1)) * sea * pltpu.roll(sea, width - 1, 1)

        wide_ref[2] = pltpu.roll(wide_ref[1], 1, 1)

        def widen(step, carry):
            base = pl.multiple_of(step * 8, 8)
            for u in range(8):
                i = base + u
                north_all[i] = jnp.broadcast_to(wide_ref[0, pl.ds(i, 1), :], (8, width))
                east_all[i] = jnp.broadcast_to(wide_ref[1, pl.ds(i, 1), :], (8, width))
                west_all[i] = jnp.broadcast_to(wide_ref[2, pl.ds(i, 1), :], (8, width))
                line = edge_ext[pl.ds(i, 1), :]
                both = jnp.where(lax.bitwise_and(lane, 7) < 4, line[:, 128:256], line[:, 256:384])
                member_all[i, :, 256:384] = pltpu.roll(
                    jnp.broadcast_to(both, (8, LANES)), 64, 1, stride=8, stride_axis=0
                )
            return carry

        lax.fori_loop(0, ext_rows // 8, widen, 0)

    member_share(source1, RIM, 0, prepare)
    edge_wait(source_copies[0])

    def covariance(source, finished):
        wide_ref[0] = joined(source[...])

        def step_rows(read, base, carry, count):
            here, flux = carry
            values = [here] + [read(base + u + 1) for u in range(count)]
            results = []
            for u in range(count):
                here, after = values[u], values[u + 1]
                flux_after = north_all[base + u] * (after - here)
                flux_east = east_all[base + u] * (pltpu.roll(here, width - 1, 1) - here)
                flux_west = west_all[base + u] * (pltpu.roll(here, 1, 1) - here)
                results.append(here + (flux_after - flux) + (flux_east + flux_west))
                flux = flux_after
            return results, (values[-1], flux)

        def first_of(read, row):
            here = read(row)
            return here, north_all[row - 1] * (here - read(row - 1))

        def sweep(read):
            def rows(step, carry):
                base = 4 + step * 24
                results, carry = step_rows(read, base, carry, 24)
                for u in range(24):
                    spread[base + u] = results[u]
                return carry

            lax.fori_loop(0, (tile_rows + 8) // 24, rows, first_of(read, 4))

        def begin(i):
            return member_all[i] * wide_ref[0, pl.ds(i, 1), :]

        def again(i):
            return spread[i]

        spread[3] = begin(3)
        spread[tile_rows + 12] = begin(tile_rows + 12)
        sweep(begin)
        for turn in range(STEPS - 2):
            sweep(again)

        carry = first_of(again, RIM)
        for part in range(mem_size):
            base = RIM + part * quarter
            results, carry = step_rows(again, base, carry, quarter)
            found = [
                jnp.sum(results[u][:, 0:256] * member_all[base + u, :, 0:256], axis=0, keepdims=True)
                for u in range(quarter)
            ]
            partial[part * quarter : (part + 1) * quarter, :] = jnp.concatenate(found, axis=0)
            finished(part)

    my_sea = lambda: coef_ext[1, pl.ds(RIM + my_rows, quarter), 0:tile_cols]
    later_part = lambda rows: partial.at[rows]
    covariance(source1, lambda part: sum_part(later_part, gathered2, 1, part))
    first_total = member_sum(later_part, gathered2, 1)
    sum_sent = sent.pop()
    first_pass = my_sea() * first_total / divisor
    source2[pl.ds(RIM + my_rows, quarter), 0:tile_cols] = kept[0] - kept[1] * first_pass
    member_share(source2, RIM, 1, lambda: edge_share(source2, send_v2, recv_v2))
    edge_wait(source_copies[1])
    sum_sent()
    covariance(source2, lambda part: sum_part(later_part, gathered3, 2, part))
    wide = my_sea() * member_sum(later_part, gathered3, 2) / divisor
    increment_ref[pl.ds(my_rows, quarter), :] = wide
    member_share(increment_ref, 0, 2)

    first, second = halves(increment_ref[...])
    lookup = jnp.concatenate([first, second], axis=0).astype(BF16)

    def look(step, carry):
        got = dot_nn(lookup, column_hot[step])
        value = got[:tile_rows] + got[tile_rows:]
        for u in range(group):
            origin = step * group + u
            high, low = slot_cells(arrived[origin])
            found = []
            for k in range(q):
                hit = rows_iota(tile_rows) == high[k : k + 1]
                start = u * span + k * LANES
                part = value[:, start : start + LANES]
                found.append(jnp.sum(jnp.where(hit, part, 0.0), axis=0, keepdims=True))
            found.append(jnp.zeros((8 - q, LANES), F32))
            answers[origin] = jnp.concatenate(found, axis=0)
        return carry

    lax.fori_loop(0, places // group, look, 0)
    exchange(answers, returned, a2a_sem.at[1])
    returned[place] = answers[place]
    exchange_wait(answers, returned, a2a_sem.at[1])
    first, second = halves(returned[...].reshape(places * 8, LANES))
    lookup = jnp.concatenate([first, second], axis=0).astype(BF16)
    answer_row = owner * 8 + lax.shift_right_logical(rank_ref[...], 7)
    got = dot_nn(lookup, lane_hot[...])
    values = got[: places * 8] + got[places * 8 :]
    for r in range(chunks):
        value = values[:, r * LANES : (r + 1) * LANES]
        hit = rows_iota(places * 8) == answer_row[r : r + 1]
        found = jnp.sum(jnp.where(hit, value, 0.0), axis=0, keepdims=True)
        residual_ref[r : r + 1, :] = depart_ref[r : r + 1, :] - found
    for wait in sent:
        wait()


def per_device(sizes, perturbations, diffusivity, sea_mask, obs_owner, obs_cell, obs_depart, obs_weight):
    lat_size, lon_size, mem_size = sizes
    members, tile_rows, tile_cols = perturbations.shape
    count = obs_cell.shape[0]
    places = lat_size * lon_size
    capacity = max(2, 2 * count // places)
    q = max(1, capacity // LANES)
    block_rows = 8
    while block_rows < 3 * q:
        block_rows *= 2
    rows = count // LANES
    ext = tile_rows + 2 * RIM
    quarter = tile_rows // mem_size
    divisor = members * mem_size - 1
    vmem = pltpu.VMEM
    dma = pltpu.SemaphoreType.DMA
    as_rows = lambda a: a.reshape(rows, LANES)
    member_rows = jnp.transpose(perturbations, (1, 0, 2)).astype(F32)
    increment, residual = pl.pallas_call(
        functools.partial(kernel, (lat_size, lon_size, mem_size, places, q, block_rows, divisor)),
        out_shape=(
            jax.ShapeDtypeStruct((tile_rows, tile_cols), F32),
            jax.ShapeDtypeStruct((rows, LANES), F32),
        ),
        in_specs=[pl.BlockSpec(memory_space=vmem)] * 8,
        out_specs=(pl.BlockSpec(memory_space=vmem),) * 2,
        scratch_shapes=[
            vmem((ext, 8, 384), F32),
            vmem((ext, 3 * LANES), F32),
            vmem((2, ext, 512), F32),
            vmem((ext, 512), F32),
            vmem((ext, 512), F32),
            vmem((ext, 8, 384), F32),
            vmem((ext, 8, 384), F32),
            vmem((ext, 8, 384), F32),
            vmem((ext, 8, 384), F32),
            vmem((places, block_rows, LANES), F32),
            vmem((places, block_rows, LANES), F32),
            vmem((2, tile_rows, tile_cols), F32),
            vmem((tile_rows, tile_cols), F32),
            vmem((mem_size, 2, quarter, tile_cols), F32),
            vmem((mem_size, quarter, tile_cols), F32),
            vmem((mem_size, quarter, tile_cols), F32),
            vmem((2, quarter, tile_cols), F32),
            vmem((places, 8, LANES), F32),
            vmem((places, 8, LANES), F32),
            vmem((rows, LANES), jnp.int32),
            vmem((4 * tile_rows, tile_cols), F32),
            vmem((3, ext, 384), F32),
            vmem((LANES, count), BF16),
            vmem((places // 4, tile_cols, 4 * q * LANES), BF16),
        ] + [dma((8,))] * 6 + [dma((8 * mem_size,)), dma((8,))] * 2 + [dma((6, 2)), dma((2, 2))],
        compiler_params=pltpu.CompilerParams(
            collective_id=0, has_side_effects=True, vmem_limit_bytes=40 * 1024 * 1024
        ),
        name="update",
    )(
        member_rows, perturbations, diffusivity, sea_mask,
        as_rows(obs_owner), as_rows(obs_cell), as_rows(obs_depart), as_rows(obs_weight),
    )
    return increment, residual.reshape(count)


def solution(mesh):
    sizes = tuple(mesh.shape[name] for name in ("lat", "lon", "mem"))
    return jax.shard_map(
        functools.partial(per_device, sizes),
        mesh=mesh,
        in_specs=(
            P("mem", "lat", "lon"),
            P("lat", "lon"),
            P("lat", "lon"),
            P(("lat", "lon", "mem"), None),
            P(("lat", "lon", "mem")),
            P(("lat", "lon", "mem")),
            P(("lat", "lon", "mem")),
        ),
        out_specs=(P("lat", "lon"), P(("lat", "lon", "mem"))),
        check_vma=False,
    )
```

```python
import functools

import jax
import jax.numpy as jnp
from jax import lax
from jax.experimental import pallas as pl
from jax.experimental.pallas import tpu as pltpu
from jax.sharding import PartitionSpec as P

STEPS = 4
LANES = 128
RIM = 8
F32 = jnp.float32
BF16 = jnp.bfloat16
MESH = pl.DeviceIdType.MESH
DIRECTIONS = [(0, 1), (0, -1), (1, 0), (-1, 0), (1, 1), (1, -1), (-1, 1), (-1, -1)]
EVERY = range(8)
SIDES = (0, 1, 4, 5, 6, 7)
AHEAD = (2, 3)
WIDE = {0: (pl.ds(0, 256), pl.ds(0, 256)), 1: (pl.ds(128, 128), pl.ds(384, 128)), -1: (pl.ds(0, 128), pl.ds(256, 128))}
NARROW = {1: (pl.ds(0, 128), pl.ds(256, 128)), -1: (pl.ds(0, 128), pl.ds(128, 128))}


def halves(value):
    high = value.astype(BF16).astype(F32)
    return high, value - high


def dot_nt(left, right):
    return lax.dot_general(left, right, (((1,), (1,)), ((), ())), preferred_element_type=F32)


def dot_nn(left, right):
    return lax.dot_general(left, right, (((1,), (0,)), ((), ())), preferred_element_type=F32)


def rows_iota(count):
    return lax.broadcasted_iota(jnp.int32, (count, LANES), 0)


def one_hot(index_row, count):
    return jnp.where(rows_iota(count) == index_row, 1.0, 0.0).astype(BF16)


def kernel(
    sizes,
    plain_ref, rate_ref, sea_ref, owner_ref, cell_ref, depart_ref, weight_ref,
    increment_ref, residual_ref,
    member_all, edge_ext, coef_ext, source1, source2, spread, north_all, east_all, west_all,
    outgoing, arrived, partial1, partial, gathered1, gathered2, gathered3, kept, answers, returned,
    rank_ref, total_ref, wide_ref, lane_hot, column_hot, plain_wide,
    send_x, recv_x, send_e, recv_e, send_c, recv_c, send_v1, recv_v1, send_v2, recv_v2, sums_sem, a2a_sem,
):
    lat_size, lon_size, mem_size, places, q, block_rows, divisor = sizes
    tile_rows, tile_cols = rate_ref.shape
    chunks = owner_ref.shape[0]
    lat = lax.axis_index("lat")
    lon = lax.axis_index("lon")
    mem = lax.axis_index("mem")
    place = lat * lon_size + lon
    quarter = tile_rows // mem_size
    shift_q = q.bit_length() - 1
    shift_b = block_rows.bit_length() - 1
    end = RIM + tile_rows
    ext_rows = tile_rows + 2 * RIM

    def place_at(step):
        other = lax.rem(place + step, places)
        return other, (other // lon_size, lax.rem(other, lon_size), mem)

    def when(condition, action):
        if condition is None:
            action()
        else:
            pl.when(condition)(action)

    def neighbour(dy, dx, member):
        return lat + dy, lax.rem(lon + dx + lon_size, lon_size), member

    barrier = pltpu.get_barrier_semaphore()

    def greet(step, carry):
        pl.semaphore_signal(barrier, inc=1, device_id=place_at(step)[1], device_id_type=MESH)
        return carry

    lax.fori_loop(1, places, greet, 0)
    for step in range(1, mem_size):
        pl.semaphore_signal(
            barrier, inc=1, device_id=(lat, lon, lax.rem(mem + step, mem_size)), device_id_type=MESH
        )

    exists = {0: None, 1: lat < lat_size - 1, -1: lat > 0}
    for dy, dx in DIRECTIONS:
        for step in range(1, mem_size):
            when(exists[dy], lambda dy=dy, dx=dx, step=step: pl.semaphore_signal(
                barrier, inc=1, device_id=neighbour(dy, dx, lax.rem(mem + step, mem_size)), device_id_type=MESH
            ))

    zero_rows = jnp.zeros((RIM, 512), F32)
    for ext in (source1, source2, coef_ext.at[0], coef_ext.at[1]):
        @pl.when(lat == 0)
        def _(ext=ext):
            ext[0:RIM, :] = zero_rows

        @pl.when(lat == lat_size - 1)
        def _(ext=ext):
            ext[end:ext_rows, :] = zero_rows

    @pl.when(lat == 0)
    def _():
        member_all[0:RIM] = jnp.zeros((RIM, 8, 384), F32)
        edge_ext[0:RIM] = jnp.zeros((RIM, 3 * LANES), F32)

    @pl.when(lat == lat_size - 1)
    def _():
        member_all[end:ext_rows] = jnp.zeros((RIM, 8, 384), F32)
        edge_ext[end:ext_rows] = jnp.zeros((RIM, 3 * LANES), F32)

    member_all[0:4, :, 0:tile_cols] = jnp.zeros((4, 8, tile_cols), F32)
    member_all[end + 4 : ext_rows, :, 0:tile_cols] = jnp.zeros((4, 8, tile_cols), F32)
    lane = lax.broadcasted_iota(jnp.int32, (1, LANES), 1)
    edges = jnp.zeros((tile_rows, LANES), F32)
    for m in range(8):
        middle = 8 * (8 - m)
        first_cols = plain_ref[m, :, 0:LANES].astype(F32)
        last_cols = plain_ref[m, :, tile_cols - LANES : tile_cols].astype(F32)
        turned = pltpu.roll(jnp.where(lane < 64, first_cols, last_cols), middle, 1)
        edges = jnp.where((lane >= middle - 4) & (lane < middle + 4), turned, edges)
    edge_ext[RIM:end, 0:LANES] = edges
    coef_ext[0, RIM:end, 0:tile_cols] = rate_ref[...]
    coef_ext[1, RIM:end, 0:tile_cols] = sea_ref[...].astype(F32)

    def halo_copies(at, send_sem, recv_sem, directions, depth=RIM, cols=None):
        made = []
        for k in directions:
            dy, dx = DIRECTIONS[k]
            source_rows = {0: pl.ds(RIM, tile_rows), 1: pl.ds(end - depth, depth), -1: pl.ds(RIM, depth)}[dy]
            target_rows = {0: pl.ds(RIM, tile_rows), 1: pl.ds(RIM - depth, depth), -1: pl.ds(end, depth)}[dy]
            source_cols, target_cols = (cols or WIDE)[dx]
            copy = pltpu.make_async_remote_copy(
                src_ref=at(source_rows, source_cols),
                dst_ref=at(target_rows, target_cols),
                send_sem=send_sem.at[k],
                recv_sem=recv_sem.at[k],
                device_id=neighbour(dy, dx, mem),
                device_id_type=MESH,
            )
            sends = {0: None, 1: lat < lat_size - 1, -1: lat > 0}[dy]
            gets = {0: None, 1: lat > 0, -1: lat < lat_size - 1}[dy]
            made.append((copy, sends, gets))
        return made

    def halo_start(copies):
        for copy, sends, gets in copies:
            when(sends, lambda copy=copy: copy.start())

    sent = []

    def halo_wait(copies):
        for copy, sends, gets in copies:
            when(gets, lambda copy=copy: copy.wait_recv())
            sent.append(lambda copy=copy, sends=sends: when(sends, lambda: copy.wait_send()))

    coef_copies = halo_copies(lambda r, c: coef_ext.at[:, r, c], send_c, recv_c, EVERY)
    edge_copies = halo_copies(lambda r, c: edge_ext.at[r, c], send_e, recv_e, SIDES, cols=NARROW)
    member_copies = halo_copies(lambda r, c: member_all.at[r, :, c], send_x, recv_x, AHEAD, depth=4)
    source_copies = [
        halo_copies(lambda r, c: source1.at[r, c], send_v1, recv_v1, EVERY),
        halo_copies(lambda r, c: source2.at[r, c], send_v2, recv_v2, EVERY),
    ]

    owner = owner_ref[...]
    upper = jnp.where(
        lax.broadcasted_iota(jnp.int32, (LANES, LANES), 0)
        < lax.broadcasted_iota(jnp.int32, (LANES, LANES), 1), 1.0, 0.0,
    ).astype(BF16)
    table = jnp.concatenate([upper, jnp.ones((LANES, LANES), BF16)], axis=1)
    before = jnp.zeros((places, LANES), F32)
    match = jnp.concatenate(
        [jnp.where(rows_iota(places) == owner[r : r + 1], 1.0, 0.0) for r in range(chunks)], axis=0
    )
    counts = dot_nn(match.astype(BF16), table)
    for r in range(chunks):
        part = slice(r * places, (r + 1) * places)
        found = jnp.sum(match[part] * (counts[part, :LANES] + before), axis=0, keepdims=True)
        rank_ref[r : r + 1, :] = found.astype(jnp.int32)
        before = before + counts[part, LANES:]
    rank = rank_ref[...]
    slot_row = owner * block_rows + lax.shift_right_logical(rank, 7)
    slot_lane = lax.bitwise_and(rank, 127)

    depart = depart_ref[...]
    weight = weight_ref[...]
    cell = cell_ref[...]
    product1, product2 = halves(weight * depart)
    weight1, weight2 = halves(weight)
    cell2 = lax.bitwise_and(cell, 127)
    cell1 = (cell - cell2).astype(F32)
    cell2 = cell2.astype(F32)
    pack_rows = places * block_rows
    row = rows_iota(pack_rows)
    inner = lax.bitwise_and(row, block_rows - 1)
    field = lax.shift_right_logical(inner, shift_q)
    base_row = row - lax.shift_left(field, shift_q)
    packed = jnp.zeros((2 * pack_rows, LANES), F32)
    for r in range(0, chunks, 4):
        lefts = []
        for c in range(r, r + 4):
            s = slice(c, c + 1)
            hit = base_row == slot_row[s]
            parts = [
                jnp.where(field == 0, of_product[s], jnp.where(field == 1, of_weight[s], of_cell[s]))
                for of_product, of_weight, of_cell in ((product1, weight1, cell1), (product2, weight2, cell2))
            ]
            lefts.append(jnp.concatenate([jnp.where(hit, p, 0.0) for p in parts], axis=0).astype(BF16))
            lane_hot[:, c * LANES : (c + 1) * LANES] = one_hot(slot_lane[s], LANES)
        right = lane_hot[:, r * LANES : (r + 4) * LANES]
        packed = packed + dot_nt(jnp.concatenate(lefts, axis=1), right)
    packed = packed[:pack_rows] + packed[pack_rows:]
    outgoing[...] = packed.reshape(places, block_rows, LANES)

    def exchange(from_ref, to_ref, sems):
        def send(step, carry):
            other, device = place_at(step)
            pltpu.make_async_remote_copy(
                src_ref=from_ref.at[other], dst_ref=to_ref.at[place],
                send_sem=sems.at[0], recv_sem=sems.at[1],
                device_id=device, device_id_type=MESH,
            ).start()
            return carry

        lax.fori_loop(1, places, send, 0)

    def exchange_wait(from_ref, to_ref, sems):
        whole = pltpu.make_async_remote_copy(
            src_ref=from_ref.at[pl.ds(0, places - 1)], dst_ref=to_ref.at[pl.ds(0, places - 1)],
            send_sem=sems.at[0], recv_sem=sems.at[1],
            device_id=place_at(1)[1], device_id_type=MESH,
        )
        whole.wait_recv()
        sent.append(whole.wait_send)

    tiles = 2 + 3 * (jnp.where(lat > 0, 1, 0) + jnp.where(lat < lat_size - 1, 1, 0))
    pl.semaphore_wait(barrier, places - 1 + (mem_size - 1) * (tiles + 1))
    exchange(outgoing, arrived, a2a_sem.at[0])
    halo_start(coef_copies)
    halo_start(edge_copies)
    for m in range(8):
        for half in range(2):
            plain_wide[half, m * tile_rows : (m + 1) * tile_rows, :] = plain_ref[
                m, :, half * LANES : (half + 1) * LANES
            ].astype(F32)

    def turn_rows(step, carry):
        for u in range(16):
            i = step * 16 + u
            for half in range(2):
                member_all[RIM + i, :, half * LANES : (half + 1) * LANES] = plain_wide[
                    half, pl.ds(i, 8, stride=tile_rows), :
                ]
        return carry

    lax.fori_loop(0, tile_rows // 16, turn_rows, 0)
    halo_start(member_copies)
    arrived[place] = outgoing[place]
    exchange_wait(outgoing, arrived, a2a_sem.at[0])

    def slot_cells(block):
        whole = block[2 * q : 3 * q].astype(jnp.int32)
        return lax.shift_right_logical(whole, 8), lax.bitwise_and(whole, 255)

    total_ref[...] = jnp.zeros_like(total_ref)
    group = 4
    span = q * LANES

    def add_blocks(step, carry):
        lefts, rights = [], []
        for u in range(group):
            block = arrived[step * group + u]
            high, low = slot_cells(block)
            for k in range(q):
                hit = rows_iota(tile_rows) == high[k : k + 1]
                parts = halves(block[k : k + 1]) + halves(block[q + k : q + k + 1])
                lefts.append(jnp.concatenate([jnp.where(hit, p, 0.0) for p in parts], axis=0).astype(BF16))
                rights.append(one_hot(low[k : k + 1], tile_cols))
        right = jnp.concatenate(rights, axis=1)
        column_hot[step] = right
        total_ref[...] += dot_nt(jnp.concatenate(lefts, axis=1), right)
        return carry

    lax.fori_loop(0, places // group, add_blocks, 0)
    for f in range(2):
        start = 2 * f * tile_rows
        partial1[f] = total_ref[start : start + tile_rows, :] + total_ref[start + tile_rows : start + 2 * tile_rows, :]

    my_rows = pl.multiple_of(mem * quarter, quarter)

    def sum_copy(part_at, got, number, other):
        sems = sums_sem.at[2 * number]
        return pltpu.make_async_remote_copy(
            src_ref=part_at(pl.ds(pl.multiple_of(other * quarter, quarter), quarter)),
            dst_ref=got.at[mem],
            send_sem=sems.at[0], recv_sem=sems.at[1],
            device_id=(lat, lon, other), device_id_type=MESH,
        )

    def sum_part(part_at, got, number, other):
        @pl.when(mem != other)
        def _():
            sum_copy(part_at, got, number, other).start()

    def member_sum(part_at, got, number):
        sems = sums_sem.at[2 * number]
        got[mem] = part_at(pl.ds(my_rows, quarter))[...]
        whole = pltpu.make_async_remote_copy(
            src_ref=got.at[pl.ds(0, mem_size - 1)], dst_ref=got.at[pl.ds(0, mem_size - 1)],
            send_sem=sems.at[0], recv_sem=sems.at[1],
            device_id=(lat, lon, lax.rem(mem + 1, mem_size)), device_id_type=MESH,
        )
        whole.wait_recv()
        sent.append(whole.wait_send)
        total = got[0]
        for other in range(1, mem_size):
            total = total + got[other]
        return total

    def edge_share(ref, send_sem, recv_sem):
        own = pl.ds(RIM + my_rows, quarter)
        for k, (dy, dx) in enumerate(DIRECTIONS):
            source_rows = {0: own, 1: pl.ds(end - RIM, RIM), -1: pl.ds(RIM, RIM)}[dy]
            target_rows = {0: own, 1: pl.ds(0, RIM), -1: pl.ds(end, RIM)}[dy]
            source_cols, target_cols = WIDE[dx]
            sends = {0: None, 1: (lat < lat_size - 1) & (mem == mem_size - 1), -1: (lat > 0) & (mem == 0)}[dy]
            for step in range(mem_size):
                copy = pltpu.make_async_remote_copy(
                    src_ref=ref.at[source_rows, source_cols], dst_ref=ref.at[target_rows, target_cols],
                    send_sem=send_sem.at[k * mem_size + step], recv_sem=recv_sem.at[k],
                    device_id=neighbour(dy, dx, lax.rem(mem + step, mem_size)), device_id_type=MESH,
                )
                when(sends, lambda copy=copy: copy.start())
                sent.append(lambda copy=copy, sends=sends: when(sends, lambda: copy.wait_send()))

    def edge_wait(copies):
        for copy, sends, gets in copies:
            when(gets, lambda copy=copy: copy.wait_recv())

    def member_share(ref, first, number, meanwhile=lambda: None):
        sems = sums_sem.at[2 * number + 1]
        mine = ref.at[pl.ds(first + my_rows, quarter), pl.ds(0, tile_cols)]
        for step in range(1, mem_size):
            pltpu.make_async_remote_copy(
                src_ref=mine, dst_ref=mine,
                send_sem=sems.at[0], recv_sem=sems.at[1],
                device_id=(lat, lon, lax.rem(mem + step, mem_size)), device_id_type=MESH,
            ).start()
        meanwhile()
        rest = ref.at[pl.ds(first, (mem_size - 1) * quarter), pl.ds(0, tile_cols)]
        whole = pltpu.make_async_remote_copy(
            src_ref=rest, dst_ref=rest, send_sem=sems.at[0], recv_sem=sems.at[1],
            device_id=(lat, lon, lax.rem(mem + 1, mem_size)), device_id_type=MESH,
        )
        whole.wait_recv()
        sent.append(whole.wait_send)

    width = 384

    def joined(value):
        side = jnp.where(lane < 64, value[..., 256:384], value[..., 384:512])
        return jnp.concatenate([value[..., 0:256], side], axis=-1)

    def face_weights():
        halo_wait(coef_copies)
        rate = joined(coef_ext[0])
        sea = joined(coef_ext[1])
        below = lambda a: jnp.concatenate([a[1:], a[:1]], axis=0)
        wide_ref[0] = 0.5 * (rate + below(rate)) * sea * below(sea)
        east = 0.5 * (rate + pltpu.roll(rate, width - 1, 1)) * sea * pltpu.roll(sea, width - 1, 1)
        wide_ref[1] = east
        wide_ref[2] = pltpu.roll(east, 1, 1)

        def widen(step, carry):
            base = pl.multiple_of(step * 8, 8)
            for u in range(8):
                i = base + u
                north_all[i] = jnp.broadcast_to(wide_ref[0, pl.ds(i, 1), :], (8, width))
                east_all[i] = jnp.broadcast_to(wide_ref[1, pl.ds(i, 1), :], (8, width))
                west_all[i] = jnp.broadcast_to(wide_ref[2, pl.ds(i, 1), :], (8, width))
            return carry

        lax.fori_loop(0, ext_rows // 8, widen, 0)

    def prepare():
        edge_share(source1, send_v1, recv_v1)
        halo_wait(edge_copies)
        halo_wait(member_copies)

        def place_sides(step, carry):
            base = pl.multiple_of(step * 16, 16)
            for u in range(16):
                i = base + u
                line = edge_ext[pl.ds(i, 1), :]
                both = jnp.where(lax.bitwise_and(lane, 7) < 4, line[:, 128:256], line[:, 256:384])
                member_all[i, :, 256:384] = pltpu.roll(
                    jnp.broadcast_to(both, (8, LANES)), 64, 1, stride=8, stride_axis=0
                )
            return carry

        lax.fori_loop(0, ext_rows // 16, place_sides, 0)

    first_part = lambda rows: partial1.at[:, rows]
    for step in range(1, mem_size):
        sum_copy(first_part, gathered1, 0, lax.rem(mem + step, mem_size)).start()
    face_weights()
    summed = member_sum(first_part, gathered1, 0)
    kept[...] = summed
    source1[pl.ds(RIM + my_rows, quarter), 0:tile_cols] = summed[0]

    member_share(source1, RIM, 0, prepare)
    edge_wait(source_copies[0])

    def covariance(source, finished):
        wide_ref[0] = joined(source[...])

        def step_rows(read, base, carry, count):
            here, flux = carry
            values = [here] + [read(base + u + 1) for u in range(count)]
            results = []
            for u in range(count):
                here, after = values[u], values[u + 1]
                flux_after = north_all[base + u] * (after - here)
                flux_east = east_all[base + u] * (pltpu.roll(here, width - 1, 1) - here)
                flux_west = west_all[base + u] * (pltpu.roll(here, 1, 1) - here)
                results.append(here + (flux_after - flux) + (flux_east + flux_west))
                flux = flux_after
            return results, (values[-1], flux)

        def first_of(read, row):
            here = read(row)
            return here, north_all[row - 1] * (here - read(row - 1))

        def sweep(read):
            def rows(step, carry):
                base = 4 + step * 24
                results, carry = step_rows(read, base, carry, 24)
                for u in range(24):
                    spread[base + u] = results[u]
                return carry

            lax.fori_loop(0, (tile_rows + 8) // 24, rows, first_of(read, 4))

        def begin(i):
            return member_all[i] * wide_ref[0, pl.ds(i, 1), :]

        def again(i):
            return spread[i]

        spread[3] = begin(3)
        spread[tile_rows + 12] = begin(tile_rows + 12)
        sweep(begin)
        for turn in range(STEPS - 2):
            sweep(again)

        carry = first_of(again, RIM)
        for part in range(mem_size):
            base = RIM + part * quarter
            results, carry = step_rows(again, base, carry, quarter)
            found = [
                jnp.sum(results[u][:, 0:256] * member_all[base + u, :, 0:256], axis=0, keepdims=True)
                for u in range(quarter)
            ]
            partial[part * quarter : (part + 1) * quarter, :] = jnp.concatenate(found, axis=0)
            finished(part)

    my_sea = lambda: coef_ext[1, pl.ds(RIM + my_rows, quarter), 0:tile_cols]
    later_part = lambda rows: partial.at[rows]
    covariance(source1, lambda part: sum_part(later_part, gathered2, 1, part))
    first_total = member_sum(later_part, gathered2, 1)
    sum_sent = sent.pop()
    first_pass = my_sea() * first_total / divisor
    source2[pl.ds(RIM + my_rows, quarter), 0:tile_cols] = kept[0] - kept[1] * first_pass
    member_share(source2, RIM, 1, lambda: edge_share(source2, send_v2, recv_v2))
    edge_wait(source_copies[1])
    sum_sent()
    covariance(source2, lambda part: sum_part(later_part, gathered3, 2, part))
    wide = my_sea() * member_sum(later_part, gathered3, 2) / divisor
    increment_ref[pl.ds(my_rows, quarter), :] = wide
    member_share(increment_ref, 0, 2)

    first, second = halves(increment_ref[...])
    lookup = jnp.concatenate([first, second], axis=0).astype(BF16)

    def look(step, carry):
        got = dot_nn(lookup, column_hot[step])
        value = got[:tile_rows] + got[tile_rows:]
        for u in range(group):
            origin = step * group + u
            high, low = slot_cells(arrived[origin])
            found = []
            for k in range(q):
                hit = rows_iota(tile_rows) == high[k : k + 1]
                start = u * span + k * LANES
                part = value[:, start : start + LANES]
                found.append(jnp.sum(jnp.where(hit, part, 0.0), axis=0, keepdims=True))
            found.append(jnp.zeros((8 - q, LANES), F32))
            answers[origin] = jnp.concatenate(found, axis=0)
        return carry

    lax.fori_loop(0, places // group, look, 0)
    exchange(answers, returned, a2a_sem.at[1])
    returned[place] = answers[place]
    exchange_wait(answers, returned, a2a_sem.at[1])
    first, second = halves(returned[...].reshape(places * 8, LANES))
    lookup = jnp.concatenate([first, second], axis=0).astype(BF16)
    answer_row = owner * 8 + lax.shift_right_logical(rank_ref[...], 7)
    got = dot_nn(lookup, lane_hot[...])
    values = got[: places * 8] + got[places * 8 :]
    for r in range(chunks):
        value = values[:, r * LANES : (r + 1) * LANES]
        hit = rows_iota(places * 8) == answer_row[r : r + 1]
        found = jnp.sum(jnp.where(hit, value, 0.0), axis=0, keepdims=True)
        residual_ref[r : r + 1, :] = depart_ref[r : r + 1, :] - found
    for wait in sent:
        wait()


def per_device(sizes, perturbations, diffusivity, sea_mask, obs_owner, obs_cell, obs_depart, obs_weight):
    lat_size, lon_size, mem_size = sizes
    members, tile_rows, tile_cols = perturbations.shape
    count = obs_cell.shape[0]
    places = lat_size * lon_size
    capacity = max(2, 2 * count // places)
    q = max(1, capacity // LANES)
    block_rows = 8
    while block_rows < 3 * q:
        block_rows *= 2
    rows = count // LANES
    ext = tile_rows + 2 * RIM
    quarter = tile_rows // mem_size
    divisor = members * mem_size - 1
    vmem = pltpu.VMEM
    dma = pltpu.SemaphoreType.DMA
    as_rows = lambda a: a.reshape(rows, LANES)
    increment, residual = pl.pallas_call(
        functools.partial(kernel, (lat_size, lon_size, mem_size, places, q, block_rows, divisor)),
        out_shape=(
            jax.ShapeDtypeStruct((tile_rows, tile_cols), F32),
            jax.ShapeDtypeStruct((rows, LANES), F32),
        ),
        in_specs=[pl.BlockSpec(memory_space=vmem)] * 7,
        out_specs=(pl.BlockSpec(memory_space=vmem),) * 2,
        scratch_shapes=[
            vmem((ext, 8, 384), F32),
            vmem((ext, 3 * LANES), F32),
            vmem((2, ext, 512), F32),
            vmem((ext, 512), F32),
            vmem((ext, 512), F32),
            vmem((ext, 8, 384), F32),
            vmem((ext, 8, 384), F32),
            vmem((ext, 8, 384), F32),
            vmem((ext, 8, 384), F32),
            vmem((places, block_rows, LANES), F32),
            vmem((places, block_rows, LANES), F32),
            vmem((2, tile_rows, tile_cols), F32),
            vmem((tile_rows, tile_cols), F32),
            vmem((mem_size, 2, quarter, tile_cols), F32),
            vmem((mem_size, quarter, tile_cols), F32),
            vmem((mem_size, quarter, tile_cols), F32),
            vmem((2, quarter, tile_cols), F32),
            vmem((places, 8, LANES), F32),
            vmem((places, 8, LANES), F32),
            vmem((rows, LANES), jnp.int32),
            vmem((4 * tile_rows, tile_cols), F32),
            vmem((3, ext, 384), F32),
            vmem((LANES, count), BF16),
            vmem((places // 4, tile_cols, 4 * q * LANES), BF16),
            vmem((2, 8 * tile_rows, LANES), F32),
        ] + [dma((8,))] * 6 + [dma((8 * mem_size,)), dma((8,))] * 2 + [dma((6, 2)), dma((2, 2))],
        compiler_params=pltpu.CompilerParams(
            collective_id=0, has_side_effects=True, vmem_limit_bytes=40 * 1024 * 1024
        ),
        name="update",
    )(
        perturbations, diffusivity, sea_mask,
        as_rows(obs_owner), as_rows(obs_cell), as_rows(obs_depart), as_rows(obs_weight),
    )
    return increment, residual.reshape(count)


def solution(mesh):
    sizes = tuple(mesh.shape[name] for name in ("lat", "lon", "mem"))
    return jax.shard_map(
        functools.partial(per_device, sizes),
        mesh=mesh,
        in_specs=(
            P("mem", "lat", "lon"),
            P("lat", "lon"),
            P("lat", "lon"),
            P(("lat", "lon", "mem"), None),
            P(("lat", "lon", "mem")),
            P(("lat", "lon", "mem")),
            P(("lat", "lon", "mem")),
        ),
        out_specs=(P("lat", "lon"), P(("lat", "lon", "mem"))),
        check_vma=False,
    )
```
